32 devices in a mesh: lon: 16 (over z, y, core), lat: 2 (over x).
Axes of the slice: x: 2, y: 2, z: 4, core: 2. Of those that a mesh axis runs over, the one named last changes fastest.
Arguments:
- node_feat: bfloat16 [16, 2, 64, 512], P('lon', 'lat'), may hold values from -6 to 6
- edge_feat: bfloat16 [16, 2, 384, 512], P('lon', 'lat'), may hold values from -6 to 6
- senders: int32 [16, 2, 384], P('lon', 'lat'), may hold values from 0 to 383, as said below
- receivers: int32 [16, 2, 384], P('lon', 'lat'), may hold values from 0 to 63
- edge_count: int32 [16, 2], P('lon', 'lat'), may hold values from 8 to 384, as said below
- halo_list: int32 [16, 2, 32], P('lon', 'lat'), may hold values from 0 to 63, as said below
- coarse_list: int32 [16, 2, 1], P('lon', 'lat'), may hold values from 0 to 63
- w_edge_in: bfloat16 [1536, 512], replicated, may hold values from -0.15625 to 0.15625
- b_edge_in: float32 [512], replicated, may hold values from -3 to 3
- w_edge_out: bfloat16 [512, 512], replicated, may hold values from -0.25 to 0.25
- gain_edge: float32 [512], replicated, may hold values from 0.1 to 1.9
- shift_edge: float32 [512], replicated, may hold values from -3 to 3
- w_node_in: bfloat16 [1024, 512], replicated, may hold values from -0.1875 to 0.1875
- b_node_in: float32 [512], replicated, may hold values from -3 to 3
- w_node_out: bfloat16 [512, 512], replicated, may hold values from -0.25 to 0.25
- gain_node: float32 [512], replicated, may hold values from 0.1 to 1.9
- shift_node: float32 [512], replicated, may hold values from -3 to 3
- cot_node: bfloat16 [16, 2, 64, 512], P('lon', 'lat'), may hold values from -6 to 6
- cot_edge: bfloat16 [16, 2, 384, 512], P('lon', 'lat'), may hold values from -6 to 6
Outputs:
- new_nodes: bfloat16 [16, 2, 64, 512], P('lon', 'lat')
- grad_nodes: bfloat16 [16, 2, 64, 512], P('lon', 'lat')
- grad_edges: bfloat16 [16, 2, 384, 512], P('lon', 'lat')
The draws below stay inside these ranges and needn't reach their ends.
Inputs may be any that keep to these rules, and one draw needn't show every extreme that they name: `senders`: A sender t < 64 is the patch's own node t; 64 <= t < 352 is border row of a neighbouring patch as in send_table, never one outside the latitude bands; larger t is a coarse-level row. `halo_list`: the 32 entries of a patch are distinct. Slots 0 to edge_count - 1 of a patch hold its edges, the rest are padding.
All inputs are finite; a program needn't handle non-finite values.
Results may differ from the reference program's by a relative error of at most 0.007.
Values may be sent and summed in bfloat16 or wider, within the bound.
No kernel may reach another device: no remote copies, remote signals or barrier semaphores. Data moves between devices by JAX's collectives and lax.ppermute only.
A program may use at most 64 MiB of HBM per device.

```python
import jax
import jax.numpy as jnp
from jax import lax

D = 512
NODE_DEV = 64
COARSE_DEV = 1
EDGE_DEV = 384
HALO = 32
PATCH_LON = 16
PATCH_LAT = 2
COARSE_ALL = 32
TABLE = 384


def draw_edge_count(key, part):
    key = jax.random.fold_in(key, 11)
    jitter_key, full_key = jax.random.split(key)
    lat_index = jax.lax.broadcasted_iota(jnp.int32, (PATCH_LON, PATCH_LAT), 1)
    polar = jnp.where((lat_index == 0) | (lat_index == PATCH_LAT - 1), 1000, 0)
    jitter = jax.random.randint(jitter_key, (PATCH_LON, PATCH_LAT), 0, 1000)
    counts = EDGE_DEV - EDGE_DEV * (jitter + polar) // 8000
    counts = jnp.maximum(counts, 8).reshape(-1)
    chosen = jax.random.randint(full_key, (), 0, PATCH_LON * PATCH_LAT)
    counts = jnp.where(jnp.arange(PATCH_LON * PATCH_LAT) == chosen, EDGE_DEV, counts)
    return counts.reshape(PATCH_LON, PATCH_LAT).astype(jnp.int32)


def draw_senders(key, part):
    key = jax.random.fold_in(key, 12)
    keys = jax.random.split(key, 7)
    shape = (PATCH_LON, PATCH_LAT, EDGE_DEV)
    category = jax.random.randint(keys[0], shape, 0, 10)
    local_pick = jax.random.randint(keys[1], shape, 0, NODE_DEV)
    lat_index = jax.lax.broadcasted_iota(jnp.int32, shape, 1)
    low_band = jnp.where(lat_index == 0, 1, 0)
    high_band = jnp.where(lat_index == PATCH_LAT - 1, 2, 3)
    lat_step = jax.random.randint(keys[2], shape, low_band, high_band)
    lon_step = jax.random.randint(keys[3], shape, 0, 3)
    pick_slot = jax.random.randint(keys[4], shape, 0, HALO)
    halo_pick = NODE_DEV + (lon_step * 3 + lat_step) * HALO + pick_slot
    coarse_pick = NODE_DEV + 9 * HALO + jax.random.randint(keys[5], shape, 0, COARSE_ALL)
    chosen_rows = jnp.where(category < 6, local_pick, jnp.where(category < 9, halo_pick, coarse_pick))
    flat_rows = chosen_rows.reshape(PATCH_LON * PATCH_LAT, EDGE_DEV)
    chosen = jax.random.randint(keys[6], (), 0, PATCH_LON * PATCH_LAT)
    corner = (jnp.arange(PATCH_LON * PATCH_LAT)[:, None] == chosen) & (jnp.arange(EDGE_DEV)[None, :] == 0)
    flat_rows = jnp.where(corner, TABLE - 1, flat_rows)
    return flat_rows.reshape(shape).astype(jnp.int32)


def draw_halo_list(key, part):
    key = jax.random.fold_in(key, 13)
    shape = (PATCH_LON, PATCH_LAT, NODE_DEV)
    scores = jax.random.randint(key, shape, 0, 1 << 20) * NODE_DEV + jax.lax.broadcasted_iota(jnp.int32, shape, 2)
    order = jnp.argsort(scores, axis=2)
    return order[:, :, :HALO].astype(jnp.int32)


def with_ends(values, own_key, least, top_value):
    shape = values.shape
    index_at = [jax.random.randint(jax.random.fold_in(own_key, axis), (), 0, shape[axis]) for axis in range(len(shape))]
    values = values.at[tuple(index_at)].set(least)
    longest = shape.index(max(shape))
    index_at[longest] = (index_at[longest] + 1) % shape[longest]
    return values.at[tuple(index_at)].set(top_value)


def level_of(own_key, extent, pieces, smallest, largest):
    def one(dim, blocks):
        draws = jax.random.uniform(jax.random.fold_in(jax.random.fold_in(own_key, 6), dim), (blocks,), jnp.float32, smallest / len(pieces), largest / len(pieces))
        return jnp.repeat(jnp.exp(draws), extent[dim] // blocks).reshape((-1,) + (1,) * (len(extent) - dim - 1))

    level = one(*pieces[0])
    for cut in pieces[1:]:
        level = level * one(*cut)
    return level


def normal_values(own_key, extent, deviation, bound, pieces=(), kind=jnp.bfloat16):
    factor_of = level_of(own_key, extent, pieces, -0.22, 0.18) if pieces else 1.0
    drawn = jax.random.normal(own_key, extent, jnp.float32) * deviation * factor_of
    return jnp.minimum(jnp.maximum(drawn, -bound), bound).astype(kind)


def setup_inputs(seed: int = 0) -> dict:
    streams_of = jax.random.split(jax.random.key(seed), 20)
    node_feat = normal_values(streams_of[0], (PATCH_LON, PATCH_LAT, NODE_DEV, D), 1.0, 6.0, ((0, 16), (1, 2)))
    edge_feat = normal_values(streams_of[1], (PATCH_LON, PATCH_LAT, EDGE_DEV, D), 1.0, 6.0, ((0, 16), (1, 2)))
    senders = draw_senders(jax.random.fold_in(streams_of[19], 71), 0)
    receivers = with_ends(jax.random.randint(streams_of[3], (PATCH_LON, PATCH_LAT, EDGE_DEV), 0, NODE_DEV), jax.random.fold_in(streams_of[3], 1), 0, NODE_DEV - 1).astype(jnp.int32)
    edge_count = draw_edge_count(jax.random.fold_in(streams_of[19], 71), 0)
    halo_list = draw_halo_list(jax.random.fold_in(streams_of[19], 71), 0)
    coarse_list = with_ends(jax.random.randint(streams_of[6], (PATCH_LON, PATCH_LAT, COARSE_DEV), 0, NODE_DEV), jax.random.fold_in(streams_of[6], 1), 0, NODE_DEV - 1).astype(jnp.int32)
    w_edge_in = normal_values(streams_of[7], (3 * D, D), (3 * D) ** -0.5, 0.15625)
    b_edge_in = normal_values(streams_of[8], (D,), 0.5, 3.0, (), jnp.float32)
    w_edge_out = normal_values(streams_of[9], (D, D), D ** -0.5, 0.25)
    gain_edge = jnp.clip(1.0 + 0.18 * jax.random.normal(streams_of[10], (D,), jnp.float32), 0.1, 1.9)
    shift_edge = normal_values(streams_of[11], (D,), 0.5, 3.0, (), jnp.float32)
    w_node_in = normal_values(streams_of[12], (2 * D, D), (2 * D) ** -0.5, 0.1875)
    b_node_in = normal_values(streams_of[13], (D,), 0.5, 3.0, (), jnp.float32)
    w_node_out = normal_values(streams_of[14], (D, D), D ** -0.5, 0.25)
    gain_node = jnp.clip(1.0 + 0.18 * jax.random.normal(streams_of[15], (D,), jnp.float32), 0.1, 1.9)
    shift_node = normal_values(streams_of[16], (D,), 0.5, 3.0, (), jnp.float32)
    cot_node = normal_values(streams_of[17], (PATCH_LON, PATCH_LAT, NODE_DEV, D), 1.0, 6.0, ((0, 16), (1, 2)))
    cot_edge = normal_values(streams_of[18], (PATCH_LON, PATCH_LAT, EDGE_DEV, D), 1.0, 6.0, ((0, 16), (1, 2)))
    return {"node_feat": node_feat, "edge_feat": edge_feat, "senders": senders, "receivers": receivers, "edge_count": edge_count, "halo_list": halo_list, "coarse_list": coarse_list, "w_edge_in": w_edge_in, "b_edge_in": b_edge_in, "w_edge_out": w_edge_out, "gain_edge": gain_edge, "shift_edge": shift_edge, "w_node_in": w_node_in, "b_node_in": b_node_in, "w_node_out": w_node_out, "gain_node": gain_node, "shift_node": shift_node, "cot_node": cot_node, "cot_edge": cot_edge}


def norm_rows(out_rows, gain, shift_vec):
    centre = out_rows - lax.optimization_barrier(jnp.mean(out_rows, axis=1, keepdims=True))
    inv_std = lax.rsqrt(lax.optimization_barrier(jnp.mean(centre * centre, axis=1, keepdims=True)) + 1e-05)
    normed = centre * inv_std
    return (normed * gain + shift_vec, normed, inv_std)

def mlp_forward(joined, w_in, b_in, w_out, gain, shift_vec):
    pre_act = jnp.dot(joined, w_in, preferred_element_type=jnp.float32) + b_in
    activation = (pre_act * jax.nn.sigmoid(pre_act)).astype(jnp.bfloat16)
    out_rows = jnp.dot(activation, w_out, preferred_element_type=jnp.float32)
    update, normed, inv_std = norm_rows(out_rows, gain, shift_vec)
    return (update, (pre_act, normed, inv_std))

def mlp_backward(cotangent, stored, w_in, w_out, gain):
    pre_act, normed, inv_std = stored
    grad_norm = cotangent * gain
    grad_out = inv_std * (grad_norm - lax.optimization_barrier(jnp.mean(grad_norm, axis=1, keepdims=True)) - normed * lax.optimization_barrier(jnp.mean(grad_norm * normed, axis=1, keepdims=True)))
    grad_act = jnp.dot(grad_out.astype(jnp.bfloat16), w_out.T, preferred_element_type=jnp.float32)
    sigmoid_val = jax.nn.sigmoid(pre_act)
    grad_pre = (grad_act * sigmoid_val * (1.0 + pre_act * (1.0 - sigmoid_val))).astype(jnp.bfloat16)
    return jnp.dot(grad_pre, w_in.T, preferred_element_type=jnp.float32)

def local_layer(node_rows, edge_rows, send_table, send_index, recv_index, live_count, w_edge_in, b_edge_in, w_edge_out, gain_edge, shift_edge, w_node_in, b_node_in, w_node_out, gain_node, shift_node, cot_node, cot_edge):
    num_nodes = node_rows.shape[0]
    num_edges = edge_rows.shape[0]
    width = node_rows.shape[1]
    live_bool = jnp.arange(num_edges, dtype=jnp.int32) < live_count
    live_mask = live_bool.astype(jnp.float32)[:, None]
    joined = jnp.concatenate([edge_rows, send_table[send_index], node_rows[recv_index]], axis=1)
    edge_upd, edge_stored = mlp_forward(joined, w_edge_in, b_edge_in, w_edge_out, gain_edge, shift_edge)
    new_edge = (edge_rows.astype(jnp.float32) + live_mask * edge_upd).astype(jnp.bfloat16)
    incidence = ((recv_index[None, :] == jnp.arange(num_nodes, dtype=jnp.int32)[:, None]) & live_bool[None, :]).astype(jnp.bfloat16)
    aggregated = jnp.dot(incidence, new_edge, preferred_element_type=jnp.float32).astype(jnp.bfloat16)
    node_join = jnp.concatenate([node_rows, aggregated], axis=1)
    node_upd, node_stored = mlp_forward(node_join, w_node_in, b_node_in, w_node_out, gain_node, shift_node)
    new_nodes = (node_rows.astype(jnp.float32) + node_upd).astype(jnp.bfloat16)
    cot_rows = cot_node.astype(jnp.float32)
    node_djoin = mlp_backward(cot_rows, node_stored, w_node_in, w_node_out, gain_node)
    edge_cot = cot_edge.astype(jnp.float32) + live_mask * node_djoin[:, width:][recv_index]
    edge_djoin = mlp_backward(live_mask * edge_cot, edge_stored, w_edge_in, w_edge_out, gain_edge)
    grad_edges = (edge_cot + edge_djoin[:, :width]).astype(jnp.bfloat16)
    table_grad = jax.ops.segment_sum(edge_djoin[:, width:2 * width], send_index, num_segments=send_table.shape[0])
    grad_local = cot_rows + node_djoin[:, :width] + jax.ops.segment_sum(edge_djoin[:, 2 * width:], recv_index, num_segments=num_nodes) + table_grad[:num_nodes]
    return (new_nodes, grad_edges, grad_local, table_grad[num_nodes:])

def reference(node_feat, edge_feat, senders, receivers, edge_count, halo_list, coarse_list, w_edge_in, b_edge_in, w_edge_out, gain_edge, shift_edge, w_node_in, b_node_in, w_node_out, gain_node, shift_node, cot_node, cot_edge):
    pick_rows = jax.vmap(jax.vmap(lambda rows_all, row_index: rows_all[row_index]))
    border = pick_rows(node_feat, halo_list)
    padded = jnp.pad(border, ((0, 0), (1, 1), (0, 0), (0, 0)))
    coarse_rows = pick_rows(node_feat, coarse_list).reshape(COARSE_ALL, D)

    def device_step(state_pair, flat_index):
        grad_all, coarse_sum = state_pair
        lon_index = flat_index // PATCH_LAT
        lat_index = flat_index % PATCH_LAT
        rim_rows = jnp.stack([padded[(lon_index + lon_step - 1) % PATCH_LON, lat_index + lat_step] for lon_step in range(3) for lat_step in range(3)])
        node_rows = node_feat[lon_index, lat_index]
        send_table = jnp.concatenate([node_rows, rim_rows.reshape(9 * HALO, D), coarse_rows], axis=0)
        new_nodes, grad_edges, grad_local, rest_grad = local_layer(node_rows, edge_feat[lon_index, lat_index], send_table, senders[lon_index, lat_index], receivers[lon_index, lat_index], edge_count[lon_index, lat_index], w_edge_in, b_edge_in, w_edge_out, gain_edge, shift_edge, w_node_in, b_node_in, w_node_out, gain_node, shift_node, cot_node[lon_index, lat_index], cot_edge[lon_index, lat_index])
        grad_all = grad_all.at[lon_index, lat_index].add(grad_local)
        rim_grad = rest_grad[:9 * HALO].reshape(9, HALO, D)
        for lon_step in range(3):
            for lat_step in range(3):
                target_lon = (lon_index + lon_step - 1) % PATCH_LON
                target_lat = lat_index + lat_step - 1
                inside = (target_lat >= 0) & (target_lat < PATCH_LAT)
                clamped = jnp.clip(target_lat, 0, PATCH_LAT - 1)
                addend = jnp.where(inside, rim_grad[3 * lon_step + lat_step], 0.0)
                grad_all = grad_all.at[target_lon, clamped, halo_list[target_lon, clamped]].add(addend)
        coarse_sum = coarse_sum + rest_grad[9 * HALO:]
        return ((grad_all, coarse_sum), (new_nodes, grad_edges))
    start_pair = (jnp.zeros(node_feat.shape, jnp.float32), jnp.zeros((COARSE_ALL, D), jnp.float32))
    flat_all = jnp.arange(PATCH_LON * PATCH_LAT, dtype=jnp.int32)
    (grad_all, coarse_sum), (new_stack, edge_stack) = lax.scan(device_step, start_pair, flat_all)
    coarse_grid = coarse_sum.reshape(PATCH_LON, PATCH_LAT, COARSE_DEV, D)
    grad_all = jax.vmap(jax.vmap(lambda grad_rows, row_index, extra: grad_rows.at[row_index].add(extra)))(grad_all, coarse_list, coarse_grid)
    new_nodes = new_stack.reshape(node_feat.shape)
    grad_edges = edge_stack.reshape(edge_feat.shape)
    return (new_nodes, grad_all.astype(jnp.bfloat16), grad_edges)
```

```python
import functools

import jax
import jax.numpy as jnp
from jax import lax
from jax.experimental import pallas as pl
from jax.experimental.pallas import tpu as pltpu
from jax.sharding import PartitionSpec as P

F32 = jnp.float32
BF16 = jnp.bfloat16
VMEM = pltpu.VMEM
SMEM = pltpu.SMEM


def dot_nn(a, b):
    return jnp.dot(a, b, preferred_element_type=F32)


def dot_tn(a, b):
    return lax.dot_general(a, b, (((0,), (0,)), ((), ())), preferred_element_type=F32)


def dot_nt(a, b):
    return lax.dot_general(a, b, (((1,), (1,)), ((), ())), preferred_element_type=F32)


def as_one_hot(mask):
    return jnp.where(mask, 1.0, 0.0).astype(BF16)


def one_hot_rows(index_row, rows):
    return lax.broadcasted_iota(jnp.int32, (rows, index_row.shape[1]), 0) == index_row


def live_one_hot(index_row, rows, count):
    lanes = lax.broadcasted_iota(jnp.int32, (rows, index_row.shape[1]), 1)
    return as_one_hot(one_hot_rows(index_row, rows) & (lanes < count))


def in_two(values):
    head = values.astype(BF16)
    tail = (values - head.astype(F32)).astype(BF16)
    return jnp.concatenate([head, tail], axis=0)


def normed_rows(out_rows):
    centre = out_rows - jnp.mean(out_rows, axis=1, keepdims=True)
    inv_std = lax.rsqrt(jnp.mean(centre * centre, axis=1, keepdims=True) + 1e-05)
    return centre * inv_std, inv_std


def norm_backward(grad_norm, normed, inv_std):
    return inv_std * (
        grad_norm
        - jnp.mean(grad_norm, axis=1, keepdims=True)
        - normed * jnp.mean(grad_norm * normed, axis=1, keepdims=True)
    )


def silu_slope(pre, sig):
    return sig * (1.0 + pre * (1.0 - sig))


class Plan:
    def __init__(self, lon, lat, nodes, edges, halo, owned, width):
        self.lon, self.lat = lon, lat
        self.nodes, self.edges, self.halo, self.owned, self.width = nodes, edges, halo, owned, width
        self.coarse = lon * lat * owned
        flat = lambda i, j: (i % lon) * lat + j
        swap = lambda pairs: [p for a, b in pairs for p in ((a, b), (b, a))]
        lat_sets = [
            [(k, k + 1) for k in range(0, lat - 1, 2)],
            [(k, k + 1) for k in range(1, lat - 1, 2)],
        ]
        self.lat_pairs = [
            swap([(flat(i, a), flat(i, b)) for i in range(lon) for a, b in pairs])
            for pairs in lat_sets
            if pairs
        ]
        self.lon_pairs = [
            swap([(flat(i, j), flat(i + 1, j)) for i in range(first, lon, 2) for j in range(lat)])
            for first in (0, 1)
        ]
        self.per_lon = 1 + len(self.lat_pairs)
        self.blocks = 3 * self.per_lon
        self.table = nodes + self.blocks * halo + self.coarse

    def positions(self, sender):
        nodes, halo = self.nodes, self.halo
        lon_odd = lax.rem(lax.axis_index("lon"), 2)
        lat_odd = lax.rem(lax.axis_index("lat"), 2)
        lon_step = [1, 2 - 2 * lon_odd, 2 * lon_odd]
        lat_step = [1, 2 - 2 * lat_odd, 2 * lat_odd][: self.per_lon]
        past = sender - (nodes + 9 * halo)
        found = jnp.where(past >= 0, past + (nodes + self.blocks * halo), sender)
        place = 0
        for a in lon_step:
            for b in lat_step:
                row = sender - (nodes + (3 * a + b) * halo)
                inside = (row >= 0) & (row < halo) & (sender >= nodes)
                found = jnp.where(inside, row + (nodes + place * halo), found)
                place += 1
        return found


def pack_kernel(plan, node, halo_list, coarse_list, border, coarse):
    rows = node[0, 0]
    border[...] = dot_tn(as_one_hot(one_hot_rows(halo_list[0], plan.nodes)), rows).astype(BF16)
    shape = (plan.coarse, plan.nodes)
    which = lax.rem(lax.broadcasted_iota(jnp.int32, shape, 0), plan.owned)
    wanted = jnp.full(shape, coarse_list[0, 0, 0], jnp.int32)
    for k in range(1, plan.owned):
        wanted = jnp.where(which == k, coarse_list[0, 0, k], wanted)
    pick = as_one_hot(lax.broadcasted_iota(jnp.int32, shape, 1) == wanted)
    coarse[...] = dot_nn(pick, rows).astype(BF16)


def ahead_kernel(
    plan, count, node, edge, receivers, w_edge_in, b_edge_in, w_node_in, b_node_in, edge_part, node_part
):
    width = plan.width
    rows = node[0, 0]
    received = live_one_hot(receivers[0], plan.nodes, count[0, 0])
    at_receiver = dot_tn(received, rows).astype(BF16)
    edge_part[...] = (
        dot_nn(edge[0, 0], w_edge_in[:width])
        + dot_nn(at_receiver, w_edge_in[2 * width :])
        + b_edge_in[...]
    )
    node_part[...] = dot_nn(rows, w_node_in[:width]) + b_node_in[...]


def main_kernel(plan, *refs):
    lats = plan.per_lon - 1
    count, node, edge, senders, receivers, border = refs[:6]
    lat_rows = refs[6 : 6 + lats]
    (
        even_rows,
        odd_rows,
        coarse_rows,
        edge_part,
        node_part,
        w_edge_in,
        w_edge_out,
        gain_edge,
        shift_edge,
        w_node_in,
        w_node_out,
        gain_node,
        shift_node,
        cot_node,
        cot_edge,
        new_nodes,
        even_grad,
        odd_grad,
        kept_grad,
        coarse_grad,
        edge_cot_out,
        edge_dpre_out,
        node_dpre_out,
        table,
    ) = refs[6 + lats :]
    nodes, halo, width = plan.nodes, plan.halo, plan.width
    start = nodes
    table[:nodes] = node[0, 0]
    for part in (border, *lat_rows, even_rows, odd_rows, coarse_rows):
        table[start : start + part.shape[0]] = part[...]
        start += part.shape[0]
    live_count = count[0, 0]
    live = jnp.where(
        lax.broadcasted_iota(jnp.int32, (plan.edges, 1), 0) < live_count, 1.0, 0.0
    ).astype(F32)
    sent = as_one_hot(one_hot_rows(plan.positions(senders[0]), plan.table))
    received = live_one_hot(receivers[0], nodes, live_count)

    at_sender = dot_tn(sent, table[...]).astype(BF16)
    edge_pre = edge_part[...] + dot_nn(at_sender, w_edge_in[width : 2 * width])
    edge_sig = jax.nn.sigmoid(edge_pre)
    edge_out = dot_nn((edge_pre * edge_sig).astype(BF16), w_edge_out[...])
    edge_normed, edge_rstd = normed_rows(edge_out)
    edge_upd = edge_normed * gain_edge[...] + shift_edge[...]
    new_edge = (edge[0, 0].astype(F32) + live * edge_upd).astype(BF16)
    aggregated = dot_nn(received, new_edge).astype(BF16)

    node_pre = node_part[...] + dot_nn(aggregated, w_node_in[width:])
    node_sig = jax.nn.sigmoid(node_pre)
    node_out = dot_nn((node_pre * node_sig).astype(BF16), w_node_out[...])
    node_normed, node_rstd = normed_rows(node_out)
    node_upd = node_normed * gain_node[...] + shift_node[...]
    new_nodes[0, 0] = (node[0, 0].astype(F32) + node_upd).astype(BF16)

    node_dout = norm_backward(
        cot_node[0, 0].astype(F32) * gain_node[...], node_normed, node_rstd
    ).astype(BF16)
    node_dpre = (dot_nt(node_dout, w_node_out[...]) * silu_slope(node_pre, node_sig)).astype(BF16)
    node_dpre_out[...] = node_dpre
    agg_grad = dot_nt(node_dpre, w_node_in[width:])
    twice = jnp.concatenate([received, received], axis=0)
    edge_cot = cot_edge[0, 0].astype(F32) + dot_tn(twice, in_two(agg_grad))
    edge_cot_out[...] = edge_cot

    edge_dout = norm_backward(live * edge_cot * gain_edge[...], edge_normed, edge_rstd).astype(BF16)
    edge_dpre = (dot_nt(edge_dout, w_edge_out[...]) * silu_slope(edge_pre, edge_sig)).astype(BF16)
    edge_dpre_out[...] = edge_dpre
    away = dot_nn(sent[nodes:], edge_dpre).astype(BF16)
    away_grad = dot_nt(away, w_edge_in[width : 2 * width])
    kept = plan.per_lon * halo
    kept_grad[...] = away_grad[:kept]
    even_grad[...] = away_grad[kept : 2 * kept].astype(BF16)
    odd_grad[...] = away_grad[2 * kept : 3 * kept].astype(BF16)
    coarse_grad[...] = away_grad[3 * kept :].astype(BF16)


def behind_kernel(
    plan,
    count,
    senders,
    receivers,
    edge_dpre,
    node_dpre,
    edge_cot,
    cot_node,
    w_edge_in,
    w_node_in,
    grad_edges,
    grad_local,
):
    width, nodes = plan.width, plan.nodes
    dpre = edge_dpre[...]
    received = live_one_hot(receivers[0], nodes, count[0, 0])
    sent = as_one_hot(one_hot_rows(senders[0], nodes))
    both = dot_nn(jnp.concatenate([sent, received], axis=0), dpre).astype(BF16)
    grad_local[...] = (
        cot_node[0, 0].astype(F32)
        + dot_nt(node_dpre[...], w_node_in[:width])
        + dot_nt(both[:nodes], w_edge_in[width : 2 * width])
        + dot_nt(both[nodes:], w_edge_in[2 * width :])
    )
    grad_edges[0, 0] = (edge_cot[...] + dot_nt(dpre, w_edge_in[:width])).astype(BF16)


def middle_kernel(plan, kept, even, odd, mine, *lat_sends):
    total = kept[...] + even[...].astype(F32) + odd[...].astype(F32)
    mine[...] = total[: plan.halo]
    for k, out in enumerate(lat_sends):
        out[...] = total[(k + 1) * plan.halo : (k + 2) * plan.halo].astype(BF16)


def last_kernel(plan, *refs):
    lats = plan.per_lon - 1
    grad_local, mine, halo_list, coarse_list, coarse = refs[:5]
    out = refs[-1]
    total = mine[...]
    for part in refs[5 : 5 + lats]:
        total = total + part[...].astype(F32)
    place = as_one_hot(one_hot_rows(halo_list[0], plan.nodes))
    result = grad_local[...] + dot_nn(jnp.concatenate([place, place], axis=1), in_two(total))
    received = coarse[...].astype(F32)
    at_row = lax.broadcasted_iota(jnp.int32, result.shape, 0)
    for k in range(plan.owned):
        terms = received
        if plan.owned > 1:
            which = lax.rem(lax.broadcasted_iota(jnp.int32, received.shape, 0), plan.owned)
            terms = jnp.where(which == k, received, 0.0)
        share = jnp.sum(terms, axis=0, keepdims=True)
        result = result + jnp.where(at_row == coarse_list[0, 0, k], share, 0.0)
    out[0, 0] = result.astype(BF16)


def call(body, name, outs, operands, smem=(), scratch=(), flops=0, mib=8):
    whole = pl.BlockSpec(memory_space=VMEM)
    scalars = pl.BlockSpec(memory_space=SMEM)
    moved = sum(a.size * a.dtype.itemsize for a in operands)
    return pl.pallas_call(
        body,
        name=name,
        out_shape=[jax.ShapeDtypeStruct(shape, dtype) for shape, dtype in outs],
        in_specs=[scalars if k in smem else whole for k in range(len(operands))],
        out_specs=[whole] * len(outs),
        scratch_shapes=list(scratch),
        compiler_params=pltpu.CompilerParams(vmem_limit_bytes=mib * 1024 * 1024),
        cost_estimate=pl.CostEstimate(flops=flops, bytes_accessed=moved, transcendentals=0),
    )(*operands)


def body(
    plan,
    node_feat,
    edge_feat,
    senders,
    receivers,
    edge_count,
    halo_list,
    coarse_list,
    w_edge_in,
    b_edge_in,
    w_edge_out,
    gain_edge,
    shift_edge,
    w_node_in,
    b_node_in,
    w_node_out,
    gain_node,
    shift_node,
    cot_node,
    cot_edge,
):
    axes = ("lon", "lat")
    halo, width, nodes, edges = plan.halo, plan.width, plan.nodes, plan.edges
    row = lambda vec: vec.reshape(1, width)
    with_plan = lambda kernel: functools.partial(kernel, plan)

    border, coarse_out = call(
        with_plan(pack_kernel),
        "pack",
        [((halo, width), BF16), ((plan.coarse, width), BF16)],
        [node_feat, halo_list, coarse_list],
        smem=(2,),
    )
    coarse_rows = lax.all_to_all(coarse_out, axes, 0, 0, tiled=True)
    lat_rows = [lax.ppermute(border, axes, pairs) for pairs in plan.lat_pairs]
    wide = jnp.concatenate([border, *lat_rows], axis=0)
    even_rows, odd_rows = [lax.ppermute(wide, axes, pairs) for pairs in plan.lon_pairs]

    edge_part, node_part = call(
        with_plan(ahead_kernel),
        "ahead",
        [((edges, width), F32), ((nodes, width), F32)],
        [edge_count, node_feat, edge_feat, receivers, w_edge_in, row(b_edge_in), w_node_in, row(b_node_in)],
        smem=(0,),
        flops=2 * (2 * edges + nodes) * width * width,
    )

    kept = plan.per_lon * halo
    new_nodes, even_grad, odd_grad, kept_grad, coarse_grad, edge_cot, edge_dpre, node_dpre = call(
        with_plan(main_kernel),
        "main",
        [
            (node_feat.shape, BF16),
            ((kept, width), BF16),
            ((kept, width), BF16),
            ((kept, width), F32),
            ((plan.coarse, width), BF16),
            ((edges, width), F32),
            ((edges, width), BF16),
            ((nodes, width), BF16),
        ],
        [
            edge_count,
            node_feat,
            edge_feat,
            senders,
            receivers,
            border,
            *lat_rows,
            even_rows,
            odd_rows,
            coarse_rows,
            edge_part,
            node_part,
            w_edge_in,
            w_edge_out,
            row(gain_edge),
            row(shift_edge),
            w_node_in,
            w_node_out,
            row(gain_node),
            row(shift_node),
            cot_node,
            cot_edge,
        ],
        smem=(0,),
        scratch=[pltpu.VMEM((plan.table, width), BF16)],
        mib=20,
        flops=2 * 5 * edges * width * width,
    )

    coarse_back = lax.all_to_all(coarse_grad, axes, 0, 0, tiled=True)
    even_back, odd_back = [
        lax.ppermute(grad, axes, pairs)
        for grad, pairs in zip((even_grad, odd_grad), plan.lon_pairs)
    ]
    grad_edges, grad_local = call(
        with_plan(behind_kernel),
        "behind",
        [(edge_feat.shape, BF16), ((nodes, width), F32)],
        [edge_count, senders, receivers, edge_dpre, node_dpre, edge_cot, cot_node, w_edge_in, w_node_in],
        smem=(0,),
        flops=2 * (edges + 3 * nodes) * width * width,
    )
    mine, *lat_sends = call(
        with_plan(middle_kernel),
        "middle",
        [((halo, width), F32)] + [((halo, width), BF16)] * len(plan.lat_pairs),
        [kept_grad, even_back, odd_back],
    )
    lat_back = [
        lax.ppermute(grad, axes, pairs) for grad, pairs in zip(lat_sends, plan.lat_pairs)
    ]
    (grad_nodes,) = call(
        with_plan(last_kernel),
        "last",
        [(node_feat.shape, BF16)],
        [grad_local, mine, halo_list, coarse_list, coarse_back, *lat_back],
        smem=(3,),
    )
    return new_nodes, grad_nodes, grad_edges


def solution(mesh):
    lon, lat = mesh.shape["lon"], mesh.shape["lat"]
    cells = lambda rank: P("lon", "lat", *([None] * (rank - 2)))

    def sharded(*args):
        node_feat, edge_feat, halo_list, coarse_list = args[0], args[1], args[5], args[6]
        plan = Plan(
            lon,
            lat,
            node_feat.shape[2],
            edge_feat.shape[2],
            halo_list.shape[2],
            coarse_list.shape[2],
            node_feat.shape[3],
        )
        return body(plan, *args)

    ranks = (4, 4, 3, 3, 2, 3, 3)
    return jax.shard_map(
        sharded,
        mesh=mesh,
        in_specs=tuple(cells(r) for r in ranks) + (P(),) * 10 + (cells(4), cells(4)),
        out_specs=(cells(4), cells(4), cells(4)),
        check_vma=False,
    )
```

```python
import functools

import jax
import jax.numpy as jnp
from jax import lax
from jax.experimental import pallas as pl
from jax.experimental.pallas import tpu as pltpu
from jax.sharding import PartitionSpec as P

F32 = jnp.float32
BF16 = jnp.bfloat16
VMEM = pltpu.VMEM


def dot_nn(a, b):
    return jnp.dot(a, b, preferred_element_type=F32)


def dot_tn(a, b):
    return lax.dot_general(a, b, (((0,), (0,)), ((), ())), preferred_element_type=F32)


def dot_nt(a, b):
    return lax.dot_general(a, b, (((1,), (1,)), ((), ())), preferred_element_type=F32)


def as_one_hot(mask):
    return jnp.where(mask, 1.0, 0.0).astype(BF16)


def one_hot_rows(index_row, rows):
    return lax.broadcasted_iota(jnp.int32, (rows, index_row.shape[1]), 0) == index_row


def live_one_hot(index_row, rows, count):
    lanes = lax.broadcasted_iota(jnp.int32, (rows, index_row.shape[1]), 1)
    return as_one_hot(one_hot_rows(index_row, rows) & (lanes < count))


def in_two(values):
    head = values.astype(BF16)
    tail = (values - head.astype(F32)).astype(BF16)
    return jnp.concatenate([head, tail], axis=0)


def normed_rows(out_rows):
    centre = out_rows - jnp.mean(out_rows, axis=1, keepdims=True)
    inv_std = lax.rsqrt(jnp.mean(centre * centre, axis=1, keepdims=True) + 1e-05)
    return centre * inv_std, inv_std


def norm_backward(grad_norm, normed, inv_std):
    return inv_std * (
        grad_norm
        - jnp.mean(grad_norm, axis=1, keepdims=True)
        - normed * jnp.mean(grad_norm * normed, axis=1, keepdims=True)
    )


def silu_slope(pre, sig):
    return sig * (1.0 + pre * (1.0 - sig))


class Moves:
    def __init__(self, sems):
        self.sems, self.used = sems, 0

    def start(self, source, target):
        copy = pltpu.make_async_copy(source, target, self.sems.at[self.used])
        self.used += 1
        copy.start()
        return copy


class Fetched:
    def __init__(self, moves, source, scratch):
        self.copy, self.scratch, self.waited = moves.start(source, scratch), scratch, False

    def __call__(self):
        if not self.waited:
            self.copy.wait()
            self.waited = True
        return self.scratch


class Plan:
    def __init__(self, lon, lat, nodes, edges, halo, owned, width):
        self.lon, self.lat = lon, lat
        self.nodes, self.edges, self.halo, self.owned, self.width = nodes, edges, halo, owned, width
        self.devices = lon * lat
        self.coarse = self.devices * owned
        flat = lambda i, j: (i % lon) * lat + j
        swap = lambda pairs: [p for a, b in pairs for p in ((a, b), (b, a))]
        lat_sets = [
            [(k, k + 1) for k in range(0, lat - 1, 2)],
            [(k, k + 1) for k in range(1, lat - 1, 2)],
        ]
        self.lat_pairs = [
            swap([(flat(i, a), flat(i, b)) for i in range(lon) for a, b in pairs])
            for pairs in lat_sets
            if pairs
        ]
        self.lon_pairs = [
            swap([(flat(i, j), flat(i + 1, j)) for i in range(first, lon, 2) for j in range(lat)])
            for first in (0, 1)
        ]
        self.per_lon = 1 + len(self.lat_pairs)
        self.blocks = 3 * self.per_lon
        self.table = nodes + self.blocks * halo + self.coarse

    def positions(self, sender):
        nodes, halo = self.nodes, self.halo
        lon_odd = lax.rem(lax.axis_index("lon"), 2)
        lat_odd = lax.rem(lax.axis_index("lat"), 2)
        lon_step = [1, 2 - 2 * lon_odd, 2 * lon_odd]
        lat_step = [1, 2 - 2 * lat_odd, 2 * lat_odd][: self.per_lon]
        past = sender - (nodes + 9 * halo)
        if self.owned > 1:
            past = jnp.where(
                past >= 0, lax.rem(past, self.owned) * self.devices + past // self.owned, past
            )
        found = jnp.where(past >= 0, past + (nodes + self.blocks * halo), sender)
        place = 0
        for a in lon_step:
            for b in lat_step:
                row = sender - (nodes + (3 * a + b) * halo)
                inside = (row >= 0) & (row < halo) & (sender >= nodes)
                found = jnp.where(inside, row + (nodes + place * halo), found)
                place += 1
        return found


def pack_kernel(plan, node, halo_list, coarse_list, border, coarse, node_s, halo_s, list_s, sems):
    moves = Moves(sems)
    node, halo_list, coarse_list = [
        Fetched(moves, *pair)
        for pair in ((node, node_s), (halo_list, halo_s), (coarse_list, list_s))
    ]
    pick = as_one_hot(one_hot_rows(halo_list()[0], plan.nodes))
    border[...] = dot_tn(pick, node()[0, 0]).astype(BF16)
    own = dot_tn(as_one_hot(one_hot_rows(coarse_list()[0], plan.nodes)), node()[0, 0])
    parts = plan.width // 128
    for k in range(plan.owned):
        for q in range(parts):
            piece = own[k : k + 1, q * 128 : (q + 1) * 128]
            coarse[:, k * parts + q, :] = jnp.broadcast_to(piece, (plan.devices, 128))


def ahead_kernel(plan, *refs):
    operands, (edge_part, node_part), scratch = refs[:8], refs[8:10], refs[10:]
    moves = Moves(scratch[-1])
    width = plan.width
    count, receivers, node, edge, w_node_in, b_node_in, w_edge_in, b_edge_in = [
        Fetched(moves, source.at[: held.shape[0]], held)
        for source, held in zip(operands, scratch[:-1])
    ]
    received = live_one_hot(receivers()[0], plan.nodes, count()[...])
    rows = node()[0, 0]
    node_part[...] = dot_nn(rows, w_node_in()[...]) + b_node_in()[...]
    at_receiver = dot_tn(received, rows).astype(BF16)
    edge_part[...] = (
        dot_nn(edge()[0, 0], w_edge_in()[:width])
        + dot_nn(at_receiver, w_edge_in()[2 * width :])
        + b_edge_in()[...]
    )


def main_kernel(plan, *refs):
    lats = plan.per_lon - 1
    total = plan.main_operands
    operands, outs, scratch = refs[:total], refs[total : total + 8], refs[total + 8 :]
    sems, table, out_vmem = scratch[-1], scratch[total], scratch[total + 1 : -1]
    moves = Moves(sems)
    nodes, halo, width = plan.nodes, plan.halo, plan.width
    start = nodes
    got = {}
    for k, (name, source) in enumerate(zip(plan.main_names, operands)):
        if name in ("w_edge_in", "w_node_in"):
            source = source.at[width : 2 * width]
        got[name] = Fetched(moves, source, scratch[k])
    count, node, edge, senders, receivers = [
        got[name] for name in ("count", "node", "edge", "senders", "receivers")
    ]
    live_count = count()[...]
    sent = as_one_hot(one_hot_rows(plan.positions(senders()[0]), plan.table))
    received = live_one_hot(receivers()[0], nodes, live_count)
    live = jnp.where(
        lax.broadcasted_iota(jnp.int32, (plan.edges, 1), 0) < live_count, 1.0, 0.0
    ).astype(F32)

    table[:nodes] = node()[0, 0]
    for name in plan.rim_names:
        part = got[name]()
        table[start : start + part.shape[0]] = part[...]
        start += part.shape[0]
    parts = width // 128
    for k in range(plan.owned):
        for q in range(parts):
            table[start : start + plan.devices, q * 128 : (q + 1) * 128] = got["coarse_rows"]()[
                :, k * parts + q, :
            ].astype(BF16)
        start += plan.devices

    at_sender = dot_tn(sent, table[...]).astype(BF16)
    edge_pre = got["edge_part"]()[...] + dot_nn(at_sender, got["w_edge_in"]()[...])
    edge_sig = jax.nn.sigmoid(edge_pre)
    edge_out = dot_nn((edge_pre * edge_sig).astype(BF16), got["w_edge_out"]()[...])
    edge_normed, edge_rstd = normed_rows(edge_out)
    edge_upd = edge_normed * got["gain_edge"]()[...] + got["shift_edge"]()[...]
    new_edge = (edge()[0, 0].astype(F32) + live * edge_upd).astype(BF16)
    aggregated = dot_nn(received, new_edge).astype(BF16)

    gain_node = got["gain_node"]()
    node_pre = got["node_part"]()[...] + dot_nn(aggregated, got["w_node_in"]()[...])
    node_sig = jax.nn.sigmoid(node_pre)
    node_out = dot_nn((node_pre * node_sig).astype(BF16), got["w_node_out"]()[...])
    node_normed, node_rstd = normed_rows(node_out)

    node_dout = norm_backward(
        got["cot_node"]()[0, 0].astype(F32) * gain_node[...], node_normed, node_rstd
    ).astype(BF16)
    node_dpre = (
        dot_nt(node_dout, got["w_node_out"]()[...]) * silu_slope(node_pre, node_sig)
    ).astype(BF16)
    agg_grad = dot_nt(node_dpre, got["w_node_in"]()[...])
    twice = jnp.concatenate([received, received], axis=0)
    edge_cot = got["cot_edge"]()[0, 0].astype(F32) + dot_tn(twice, in_two(agg_grad))

    edge_dout = norm_backward(
        live * edge_cot * got["gain_edge"]()[...], edge_normed, edge_rstd
    ).astype(BF16)
    edge_dpre = (
        dot_nt(edge_dout, got["w_edge_out"]()[...]) * silu_slope(edge_pre, edge_sig)
    ).astype(BF16)
    away = dot_nn(sent[nodes:], edge_dpre).astype(BF16)
    away_grad = dot_nt(away, got["w_edge_in"]()[...])
    kept = plan.per_lon * halo
    (even_out, odd_out, coarse_out, kept_out, new_out, cot_out, edpre_out, ndpre_out) = out_vmem
    even_out[...] = away_grad[kept : 2 * kept].astype(BF16)
    odd_out[...] = away_grad[2 * kept : 3 * kept].astype(BF16)
    start = 3 * kept
    for k in range(plan.owned):
        for q in range(parts):
            coarse_out[:, k * parts + q, :] = away_grad[
                start : start + plan.devices, q * 128 : (q + 1) * 128
            ]
        start += plan.devices
    copies = [moves.start(out_vmem[k], outs[k]) for k in range(3)]
    kept_out[...] = away_grad[:kept]
    node_upd = node_normed * gain_node[...] + got["shift_node"]()[...]
    new_out[0, 0] = (node()[0, 0].astype(F32) + node_upd).astype(BF16)
    cot_out[...] = edge_cot
    edpre_out[...] = edge_dpre
    ndpre_out[...] = node_dpre
    copies += [moves.start(out_vmem[k], outs[k]) for k in range(3, 8)]
    for copy in copies:
        copy.wait()


def behind_kernel(plan, *refs):
    operands, (grad_edges, grad_local), scratch = refs[:9], refs[9:11], refs[11:]
    moves = Moves(scratch[-1])
    (
        count,
        senders,
        receivers,
        edge_dpre,
        node_dpre,
        cot_node,
        w_node_in,
        edge_cot,
        w_edge_in,
    ) = [
        Fetched(moves, source.at[: held.shape[0]], held)
        for source, held in zip(operands, scratch[:-1])
    ]
    width, nodes = plan.width, plan.nodes
    received = live_one_hot(receivers()[0], nodes, count()[...])
    sent = as_one_hot(one_hot_rows(senders()[0], nodes))
    dpre = edge_dpre()[...]
    both = dot_nn(jnp.concatenate([sent, received], axis=0), dpre).astype(BF16)
    from_node = dot_nt(node_dpre()[...], w_node_in()[...])
    weights = w_edge_in()
    grad_local[...] = (
        cot_node()[0, 0].astype(F32)
        + from_node
        + dot_nt(both[:nodes], weights[width : 2 * width])
        + dot_nt(both[nodes:], weights[2 * width :])
    )
    grad_edges[0, 0] = (edge_cot()[...] + dot_nt(dpre, weights[:width])).astype(BF16)


def join_kernel(*refs):
    start = 0
    for part in refs[:-1]:
        refs[-1][start : start + part.shape[0]] = part[...]
        start += part.shape[0]


def middle_kernel(plan, kept, even, odd, mine, *lat_sends):
    total = kept[...] + even[...].astype(F32) + odd[...].astype(F32)
    mine[...] = total[: plan.halo]
    for k, out in enumerate(lat_sends):
        out[...] = total[(k + 1) * plan.halo : (k + 2) * plan.halo].astype(BF16)


def last_kernel(plan, *refs):
    lats = plan.per_lon - 1
    grad_local, mine, halo_list, coarse_list, coarse = refs[:5]
    out = refs[-1]
    total = mine[...]
    for part in refs[5 : 5 + lats]:
        total = total + part[...].astype(F32)
    place = as_one_hot(one_hot_rows(halo_list[0], plan.nodes))
    result = grad_local[...] + dot_nn(jnp.concatenate([place, place], axis=1), in_two(total))
    share = jnp.sum(coarse[...], axis=0)
    at_row = lax.broadcasted_iota(jnp.int32, (plan.nodes, 1), 0)
    parts = plan.width // 128
    for k in range(plan.owned):
        row = jnp.concatenate([share[k * parts + q : k * parts + q + 1] for q in range(parts)], axis=1)
        result = result + jnp.where(at_row == coarse_list[0, :, k : k + 1], row, 0.0)
    out[0, 0] = result.astype(BF16)


def call(body, name, outs, operands, scratch=(), flops=0, mib=8, copied=False):
    whole = pl.BlockSpec(memory_space=VMEM)
    moved = sum(a.size * a.dtype.itemsize for a in operands)
    return pl.pallas_call(
        body,
        name=name,
        out_shape=[jax.ShapeDtypeStruct(shape, dtype) for shape, dtype in outs],
        in_specs=[pl.BlockSpec(memory_space=pl.ANY) if scratch else whole] * len(operands),
        out_specs=[pl.BlockSpec(memory_space=pl.ANY) if copied else whole] * len(outs),
        scratch_shapes=list(scratch),
        compiler_params=pltpu.CompilerParams(vmem_limit_bytes=mib * 1024 * 1024),
        cost_estimate=pl.CostEstimate(flops=flops, bytes_accessed=moved, transcendentals=0),
    )(*operands)


def like(arrays, cut=-1):
    return [
        pltpu.VMEM((a.shape[0] // 2 if k == cut else a.shape[0],) + a.shape[1:], a.dtype)
        for k, a in enumerate(arrays)
    ]


def sems(count):
    return pltpu.SemaphoreType.DMA((count,))


def body(
    plan,
    node_feat,
    edge_feat,
    senders,
    receivers,
    edge_count,
    halo_list,
    coarse_list,
    w_edge_in,
    b_edge_in,
    w_edge_out,
    gain_edge,
    shift_edge,
    w_node_in,
    b_node_in,
    w_node_out,
    gain_node,
    shift_node,
    cot_node,
    cot_edge,
):
    axes = ("lon", "lat")
    halo, width, nodes, edges = plan.halo, plan.width, plan.nodes, plan.edges
    row = lambda vec: vec.reshape(1, width)
    with_plan = lambda kernel: functools.partial(kernel, plan)
    coarse_shape = (plan.devices, plan.owned * width // 128, 128)

    operands = [node_feat, halo_list, coarse_list]
    border, coarse_out = call(
        with_plan(pack_kernel),
        "pack",
        [((halo, width), BF16), (coarse_shape, F32)],
        operands,
        scratch=like(operands) + [sems(3)],
        mib=56,
    )
    coarse_rows = lax.all_to_all(coarse_out, axes, 0, 0, tiled=True)
    lat_rows = [lax.ppermute(border, axes, pairs) for pairs in plan.lat_pairs]
    (wide,) = call(
        join_kernel, "join", [((plan.per_lon * halo, width), BF16)], [border, *lat_rows]
    )
    even_rows, odd_rows = [lax.ppermute(wide, axes, pairs) for pairs in plan.lon_pairs]

    operands = [
        edge_count,
        receivers,
        node_feat,
        edge_feat,
        w_node_in,
        row(b_node_in),
        w_edge_in,
        row(b_edge_in),
    ]
    edge_part, node_part = call(
        with_plan(ahead_kernel),
        "ahead",
        [((edges, width), F32), ((nodes, width), F32)],
        operands,
        scratch=like(operands, 4) + [sems(len(operands))],
        flops=2 * (2 * edges + nodes) * width * width,
        mib=56,
    )

    kept = plan.per_lon * halo
    named = {
        "count": edge_count,
        "senders": senders,
        "receivers": receivers,
        "node": node_feat,
        "wide": wide,
        "even_rows": even_rows,
        "odd_rows": odd_rows,
        "coarse_rows": coarse_rows,
        "w_edge_in": w_edge_in,
        "edge_part": edge_part,
        "w_edge_out": w_edge_out,
        "gain_edge": row(gain_edge),
        "shift_edge": row(shift_edge),
        "edge": edge_feat,
        "w_node_in": w_node_in,
        "node_part": node_part,
        "w_node_out": w_node_out,
        "gain_node": row(gain_node),
        "cot_node": cot_node,
        "cot_edge": cot_edge,
        "shift_node": row(shift_node),
    }
    plan.main_names = list(named)
    plan.rim_names = ["wide", "even_rows", "odd_rows"]
    plan.main_operands = len(named)
    outs = [
        ((kept, width), BF16),
        ((kept, width), BF16),
        (coarse_shape, F32),
        ((kept, width), F32),
        (node_feat.shape, BF16),
        ((edges, width), F32),
        ((edges, width), BF16),
        ((nodes, width), BF16),
    ]
    operands = list(named.values())
    parts_of = {"w_edge_in": (width, width), "w_node_in": (width, width)}
    even_grad, odd_grad, coarse_grad, kept_grad, new_nodes, edge_cot, edge_dpre, node_dpre = call(
        with_plan(main_kernel),
        "main",
        outs,
        operands,
        scratch=[
            pltpu.VMEM(parts_of.get(name, a.shape), a.dtype) for name, a in named.items()
        ]
        + [pltpu.VMEM((plan.table, width), BF16)]
        + [pltpu.VMEM(shape, dtype) for shape, dtype in outs]
        + [sems(len(named) + len(outs))],
        flops=2 * 5 * edges * width * width,
        mib=56,
        copied=True,
    )

    coarse_back = lax.all_to_all(coarse_grad, axes, 0, 0, tiled=True)
    even_back, odd_back = [
        lax.ppermute(grad, axes, pairs)
        for grad, pairs in zip((even_grad, odd_grad), plan.lon_pairs)
    ]
    operands = [
        edge_count,
        senders,
        receivers,
        edge_dpre,
        node_dpre,
        cot_node,
        w_node_in,
        edge_cot,
        w_edge_in,
    ]
    grad_edges, grad_local = call(
        with_plan(behind_kernel),
        "behind",
        [(edge_feat.shape, BF16), ((nodes, width), F32)],
        operands,
        scratch=like(operands, 6) + [sems(len(operands))],
        flops=2 * (edges + 3 * nodes) * width * width,
        mib=56,
    )
    mine, *lat_sends = call(
        with_plan(middle_kernel),
        "middle",
        [((halo, width), F32)] + [((halo, width), BF16)] * len(plan.lat_pairs),
        [kept_grad, even_back, odd_back],
    )
    lat_back = [
        lax.ppermute(grad, axes, pairs) for grad, pairs in zip(lat_sends, plan.lat_pairs)
    ]
    (grad_nodes,) = call(
        with_plan(last_kernel),
        "last",
        [(node_feat.shape, BF16)],
        [grad_local, mine, halo_list, coarse_list, coarse_back, *lat_back],
    )
    return new_nodes, grad_nodes, grad_edges


def solution(mesh):
    lon, lat = mesh.shape["lon"], mesh.shape["lat"]
    cells = lambda rank: P("lon", "lat", *([None] * (rank - 2)))

    def sharded(*args):
        node_feat, edge_feat, halo_list, coarse_list = args[0], args[1], args[5], args[6]
        plan = Plan(
            lon,
            lat,
            node_feat.shape[2],
            edge_feat.shape[2],
            halo_list.shape[2],
            coarse_list.shape[2],
            node_feat.shape[3],
        )
        return body(plan, *args)

    ranks = (4, 4, 3, 3, 2, 3, 3)
    return jax.shard_map(
        sharded,
        mesh=mesh,
        in_specs=tuple(cells(r) for r in ranks) + (P(),) * 10 + (cells(4), cells(4)),
        out_specs=(cells(4), cells(4), cells(4)),
        check_vma=False,
    )
```

```python
import functools

import jax
import jax.numpy as jnp
from jax import lax
from jax.experimental import pallas as pl
from jax.experimental.pallas import tpu as pltpu
from jax.sharding import PartitionSpec as P

F32 = jnp.float32
BF16 = jnp.bfloat16
VMEM = pltpu.VMEM
SENT_ROWS = 128


def dot_nn(a, b):
    return jnp.dot(a, b, preferred_element_type=F32)


def dot_tn(a, b):
    return lax.dot_general(a, b, (((0,), (0,)), ((), ())), preferred_element_type=F32)


def dot_nt(a, b):
    return lax.dot_general(a, b, (((1,), (1,)), ((), ())), preferred_element_type=F32)


def as_one_hot(mask):
    return jnp.where(mask, 1.0, 0.0).astype(BF16)


def one_hot_rows(index_row, rows):
    return lax.broadcasted_iota(jnp.int32, (rows, index_row.shape[1]), 0) == index_row


def live_one_hot(index_row, rows, count):
    lanes = lax.broadcasted_iota(jnp.int32, (rows, index_row.shape[1]), 1)
    return as_one_hot(one_hot_rows(index_row, rows) & (lanes < count))


def in_two(values):
    head = values.astype(BF16)
    tail = (values - head.astype(F32)).astype(BF16)
    return jnp.concatenate([head, tail], axis=0)


def normed_rows(out_rows):
    centre = out_rows - jnp.mean(out_rows, axis=1, keepdims=True)
    inv_std = lax.rsqrt(jnp.mean(centre * centre, axis=1, keepdims=True) + 1e-05)
    return centre * inv_std, inv_std


def norm_backward(grad_norm, normed, inv_std):
    return inv_std * (
        grad_norm
        - jnp.mean(grad_norm, axis=1, keepdims=True)
        - normed * jnp.mean(grad_norm * normed, axis=1, keepdims=True)
    )


def silu_slope(pre, sig):
    return sig * (1.0 + pre * (1.0 - sig))


class Moves:
    def __init__(self, sems):
        self.sems, self.used = sems, 0

    def start(self, source, target):
        copy = pltpu.make_async_copy(source, target, self.sems.at[self.used])
        self.used += 1
        copy.start()
        return copy


class Plan:
    def __init__(self, lon, lat, nodes, edges, halo, owned, width):
        self.lon, self.lat = lon, lat
        self.nodes, self.edges, self.halo, self.owned, self.width = nodes, edges, halo, owned, width
        self.devices = lon * lat
        self.coarse = self.devices * owned
        flat = lambda i, j: (i % lon) * lat + j
        swap = lambda pairs: [p for a, b in pairs for p in ((a, b), (b, a))]
        lat_sets = [
            [(k, k + 1) for k in range(0, lat - 1, 2)],
            [(k, k + 1) for k in range(1, lat - 1, 2)],
        ]
        self.lat_pairs = [
            swap([(flat(i, a), flat(i, b)) for i in range(lon) for a, b in pairs])
            for pairs in lat_sets
            if pairs
        ]
        self.lon_pairs = [
            swap([(flat(i, j), flat(i + 1, j)) for i in range(first, lon, 2) for j in range(lat)])
            for first in (0, 1)
        ]
        self.per_lon = 1 + len(self.lat_pairs)
        self.blocks = 3 * self.per_lon
        self.table = nodes + self.blocks * halo + self.coarse

    def positions(self, sender):
        nodes, halo = self.nodes, self.halo
        lon_odd = lax.rem(lax.axis_index("lon"), 2)
        lat_odd = lax.rem(lax.axis_index("lat"), 2)
        lon_step = [1, 2 - 2 * lon_odd, 2 * lon_odd]
        lat_step = [1, 2 - 2 * lat_odd, 2 * lat_odd][: self.per_lon]
        past = sender - (nodes + 9 * halo)
        if self.owned > 1:
            past = jnp.where(
                past >= 0, lax.rem(past, self.owned) * self.devices + past // self.owned, past
            )
        found = jnp.where(past >= 0, past + (nodes + self.blocks * halo), sender)
        place = 0
        for a in lon_step:
            for b in lat_step:
                row = sender - (nodes + (3 * a + b) * halo)
                inside = (row >= 0) & (row < halo) & (sender >= nodes)
                found = jnp.where(inside, row + (nodes + place * halo), found)
                place += 1
        return found


def pack_kernel(plan, node, halo_list, coarse_list, border, coarse, node_s, halo_s, list_s, sems):
    moves = Moves(sems)
    pairs = ((coarse_list, list_s), (halo_list, halo_s), (node, node_s))
    for copy in [moves.start(*pair) for pair in pairs]:
        copy.wait()
    rows = node_s[0, 0]
    pick = as_one_hot(one_hot_rows(halo_s[0], plan.nodes))
    border[: plan.halo] = dot_tn(pick, rows).astype(BF16)
    own = dot_tn(as_one_hot(one_hot_rows(list_s[0], plan.nodes)), rows)
    parts = plan.width // 128
    for k in range(plan.owned):
        for q in range(parts):
            piece = own[k : k + 1, q * 128 : (q + 1) * 128]
            coarse[:, k * parts + q, :] = jnp.broadcast_to(piece, (plan.devices, 128))


def block_of(ref, part, width):
    return ref if part is None else ref.at[pl.ds(part * width, width)]


def ahead_kernel(plan, *refs):
    operands = dict(zip(plan.ahead_in, refs))
    refs = refs[len(plan.ahead_in) :]
    held = dict(zip(plan.ahead_out, refs))
    sems = refs[-1]
    held.update(zip(plan.ahead_held, refs[len(plan.ahead_out) : -1]))
    moves = Moves(sems)
    width, nodes = plan.width, plan.nodes
    copies = {
        name: moves.start(block_of(operands[source], part, width), held[name])
        for name, (source, part) in plan.ahead_copies.items()
    }

    def got(name):
        if name in copies:
            copies.pop(name).wait()
        return held[name]

    count = got("count")[...]
    received = live_one_hot(got("receivers")[0], nodes, count)
    held["received"][...] = received
    held["sent"][...] = as_one_hot(
        one_hot_rows(plan.positions(got("senders")[0]), plan.table)
    )
    place = as_one_hot(one_hot_rows(got("halo_list")[0], nodes))
    held["place"][...] = jnp.concatenate([place, place], axis=1)
    at_coarse = one_hot_rows(got("coarse_list")[0], nodes)
    held["at_coarse"][...] = jnp.where(at_coarse, 1.0, 0.0).astype(F32)
    rows = got("node")[0, 0]
    at_receiver = dot_tn(received, rows).astype(BF16)
    held["edge_part"][...] = (
        dot_nn(got("edge")[0, 0], got("w_edge_top")[...])
        + dot_nn(at_receiver, got("w_edge_low")[...])
        + got("b_edge_in")[...]
    )
    held["node_part"][...] = dot_nn(rows, got("w_node_top")[...]) + got("b_node_in")[...]
    for copy in copies.values():
        copy.wait()


def join_kernel(plan, *refs):
    for k, part in enumerate(refs[:-1]):
        refs[-1][k * plan.halo : (k + 1) * plan.halo] = part[: plan.halo]


def gather_kernel(plan, rows, _, coarse):
    parts = plan.width // 128
    for k in range(plan.owned):
        for q in range(parts):
            coarse[:, k * parts + q, :] = rows[
                k * plan.devices : (k + 1) * plan.devices, q * 128 : (q + 1) * 128
            ]


def edge_cotangent(cot_edge, received, agg_grad):
    twice = jnp.concatenate([received, received], axis=0)
    return cot_edge[0, 0].astype(F32) + dot_tn(twice, agg_grad)


def main_kernel(plan, *refs):
    here = dict(zip(plan.main_names, refs))
    refs = refs[len(plan.main_names) :]
    even_grad, odd_grad, coarse_grad, kept_grad, agg_out, edge_dpre_out, local = refs[:7]
    new_nodes, table, new_s = refs[7:10]
    sems, held = refs[-1], dict(zip(plan.main_held, refs[10:-1]))
    nodes, halo, width = plan.nodes, plan.halo, plan.width
    sent, received = here["sent"], here["received"][...]
    live = jnp.where(
        lax.broadcasted_iota(jnp.int32, (plan.edges, 1), 0) < here["count"][0, 0], 1.0, 0.0
    ).astype(F32)
    moves = Moves(sems)
    copies = {
        name: moves.start(block_of(here[source], part, width), held[name])
        for name, (source, part) in plan.main_copies.items()
    }

    def got(name):
        if name in copies:
            copies.pop(name).wait()
        return held[name] if name in held else here[name]

    start = nodes
    table[:nodes] = got("node")[0, 0]
    for name in ("wide", "even_rows", "odd_rows"):
        rim = plan.per_lon * halo
        table[start : start + rim] = got(name)[:rim]
        start += rim
    parts = width // 128
    for k in range(plan.owned):
        for q in range(parts):
            table[start : start + plan.devices, q * 128 : (q + 1) * 128] = got("coarse_rows")[
                :, k * parts + q, :
            ].astype(BF16)
        start += plan.devices

    w_edge_mid = got("w_edge_mid")[...]
    at_sender = dot_tn(sent[...], table[...]).astype(BF16)
    edge_pre = got("edge_part")[...] + dot_nn(at_sender, w_edge_mid)
    edge_sig = jax.nn.sigmoid(edge_pre)
    edge_out = dot_nn((edge_pre * edge_sig).astype(BF16), got("w_edge_out")[...])
    edge_normed, edge_rstd = normed_rows(edge_out)
    edge_upd = edge_normed * got("gain_edge")[...] + got("shift_edge")[...]
    new_edge = (got("edge")[0, 0].astype(F32) + live * edge_upd).astype(BF16)
    aggregated = dot_nn(received, new_edge).astype(BF16)

    node_pre = got("node_part")[...] + dot_nn(aggregated, got("w_node_low")[...])
    node_sig = jax.nn.sigmoid(node_pre)
    node_out = dot_nn((node_pre * node_sig).astype(BF16), got("w_node_out")[...])
    node_normed, node_rstd = normed_rows(node_out)
    node_upd = node_normed * got("gain_node")[...] + got("shift_node")[...]
    new_s[0, 0] = (got("node")[0, 0].astype(F32) + node_upd).astype(BF16)
    leaving = moves.start(new_s, new_nodes)

    node_dout = norm_backward(
        got("cot_node")[0, 0].astype(F32) * got("gain_node")[...], node_normed, node_rstd
    ).astype(BF16)
    node_dpre = (
        dot_nt(node_dout, got("w_node_out")[...]) * silu_slope(node_pre, node_sig)
    ).astype(BF16)
    agg_grad = in_two(dot_nt(node_dpre, got("w_node_low")[...]))
    agg_out[...] = agg_grad
    edge_cot = edge_cotangent(got("cot_edge"), received, agg_grad)

    edge_dout = norm_backward(
        live * edge_cot * got("gain_edge")[...], edge_normed, edge_rstd
    ).astype(BF16)
    edge_dpre = (
        dot_nt(edge_dout, got("w_edge_out")[...]) * silu_slope(edge_pre, edge_sig)
    ).astype(BF16)
    edge_dpre_out[...] = edge_dpre
    away_grad = dot_nt(dot_nn(sent[...], edge_dpre).astype(BF16), w_edge_mid)
    own_grad, away_grad = away_grad[:nodes], away_grad[nodes:]
    kept = plan.per_lon * halo
    kept_grad[...] = away_grad[:kept]
    even_grad[:kept] = away_grad[kept : 2 * kept].astype(BF16)
    odd_grad[:kept] = away_grad[2 * kept : 3 * kept].astype(BF16)
    coarse_grad[...] = away_grad[3 * kept :]
    local[...] = (
        got("cot_node")[0, 0].astype(F32) + dot_nt(node_dpre, got("w_node_top")[...]) + own_grad
    )
    leaving.wait()


def behind_kernel(plan, *refs):
    received, edge_dpre, agg_grad, local, _, w_edge_in, cot_edge, grad_local, grad_edges = refs[:9]
    w_top_s, w_low_s, cot_s, grad_s, sems = refs[9:]
    moves, width = Moves(sems), plan.width
    top = moves.start(block_of(w_edge_in, 0, width), w_top_s)
    cot = moves.start(cot_edge, cot_s)
    low = moves.start(block_of(w_edge_in, 2, width), w_low_s)
    dpre = edge_dpre[...]
    at_receiver = dot_nn(received[...], dpre).astype(BF16)
    cot.wait()
    edge_cot = edge_cotangent(cot_s, received[...], agg_grad[...])
    top.wait()
    grad_s[0, 0] = (edge_cot + dot_nt(dpre, w_top_s[...])).astype(BF16)
    leaving = moves.start(grad_s, grad_edges)
    low.wait()
    grad_local[...] = local[...] + dot_nt(at_receiver, w_low_s[...])
    leaving.wait()


def middle_kernel(plan, kept, even, odd, mine, *lat_sends):
    rows = kept.shape[0]
    total = kept[...] + even[:rows].astype(F32) + odd[:rows].astype(F32)
    mine[...] = total[: plan.halo]
    for k, out in enumerate(lat_sends):
        out[...] = total[(k + 1) * plan.halo : (k + 2) * plan.halo].astype(BF16)


def last_kernel(plan, *refs):
    grad_local, mine, place, at_coarse, coarse = refs[:5]
    out = refs[-1]
    total = mine[...]
    for part in refs[5:-1]:
        total = total + part[...].astype(F32)
    result = grad_local[...] + dot_nn(place[...], in_two(total))
    share = jnp.sum(coarse[...], axis=0)
    parts = plan.width // 128
    for k in range(plan.owned):
        row = jnp.concatenate([share[k * parts + q : k * parts + q + 1] for q in range(parts)], axis=1)
        result = result + at_coarse[:, k : k + 1] * row
    out[0, 0] = result.astype(BF16)


def call(body, name, outs, operands, far=(), scratch=(), flops=0, mib=4, results=0):
    whole = pl.BlockSpec(memory_space=VMEM)
    scalars = pl.BlockSpec(memory_space=pltpu.SMEM)
    anywhere = pl.BlockSpec(memory_space=pl.ANY)
    far = [pltpu.with_memory_space_constraint(a, pltpu.HBM) if a.size > 1 else a for a in far]
    moved = sum(a.size * a.dtype.itemsize for a in (*operands, *far))
    near = len(outs) - results
    return pl.pallas_call(
        body,
        name=name,
        out_shape=[VMEM(shape, dtype) for shape, dtype in outs[:near]]
        + [jax.ShapeDtypeStruct(shape, dtype) for shape, dtype in outs[near:]],
        in_specs=[scalars if a.size == 1 else whole for a in operands] + [anywhere] * len(far),
        out_specs=[whole] * near + [anywhere if scratch else whole] * results,
        scratch_shapes=list(scratch),
        compiler_params=pltpu.CompilerParams(vmem_limit_bytes=mib * 1024 * 1024),
        cost_estimate=pl.CostEstimate(flops=flops, bytes_accessed=moved, transcendentals=0),
    )(*operands, *far)


def like(arrays):
    return [VMEM(a.shape, a.dtype) for a in arrays]


def sems(count):
    return pltpu.SemaphoreType.DMA((count,))


def body(
    plan,
    node_feat,
    edge_feat,
    senders,
    receivers,
    edge_count,
    halo_list,
    coarse_list,
    w_edge_in,
    b_edge_in,
    w_edge_out,
    gain_edge,
    shift_edge,
    w_node_in,
    b_node_in,
    w_node_out,
    gain_node,
    shift_node,
    cot_node,
    cot_edge,
):
    axes = ("lon", "lat")
    halo, width, nodes, edges = plan.halo, plan.width, plan.nodes, plan.edges
    row = lambda vec: vec.reshape(1, width)
    with_plan = lambda kernel: functools.partial(kernel, plan)
    coarse_shape = (plan.devices, plan.owned * width // 128, 128)
    kept = plan.per_lon * halo

    operands = [node_feat, halo_list, coarse_list]
    border, coarse_out = call(
        with_plan(pack_kernel),
        "pack",
        [((max(halo, SENT_ROWS), width), BF16), (coarse_shape, F32)],
        [],
        far=operands,
        scratch=like(operands) + [sems(3)],
    )
    coarse_rows = lax.all_to_all(coarse_out, axes, 0, 0, tiled=True)
    lat_rows = [lax.ppermute(border, axes, pairs) for pairs in plan.lat_pairs]

    far = {
        "count": edge_count,
        "receivers": receivers,
        "node": node_feat,
        "edge": edge_feat,
        "w_edge_in": w_edge_in,
        "b_edge_in": row(b_edge_in),
        "senders": senders,
        "halo_list": halo_list,
        "coarse_list": coarse_list,
        "w_node_in": w_node_in,
        "b_node_in": row(b_node_in),
    }
    square = ((width, width), BF16)
    copies = {name: (name, None) for name in far if name not in ("w_edge_in", "w_node_in")}
    copies["w_edge_top"] = ("w_edge_in", 0)
    copies["w_edge_low"] = ("w_edge_in", 2)
    copies["w_node_top"] = ("w_node_in", 0)
    copies["w_edge_mid"] = ("w_edge_in", 1)
    outs = {
        "w_edge_mid": square,
        "edge_part": ((edges, width), F32),
        "node_part": ((nodes, width), F32),
        "sent": ((plan.table, edges), BF16),
        "received": ((nodes, edges), BF16),
        "place": ((nodes, 2 * halo), BF16),
        "at_coarse": ((nodes, plan.owned), F32),
    }
    held = {
        name: square if part is not None else (far[source].shape, far[source].dtype)
        for name, (source, part) in copies.items()
        if name not in outs
    }
    plan.ahead_in, plan.ahead_out, plan.ahead_held = list(far), list(outs), list(held)
    plan.ahead_copies = copies
    at = dict(
        zip(
            outs,
            call(
                with_plan(ahead_kernel),
                "ahead",
                list(outs.values()),
                [],
                far=list(far.values()),
                scratch=[VMEM(*kind) for kind in held.values()] + [sems(len(copies))],
                flops=2 * (2 * edges + nodes) * width * width,
                mib=12,
            ),
        )
    )

    (wide,) = call(with_plan(join_kernel), "join", [((kept, width), BF16)], [border, *lat_rows])
    even_rows, odd_rows = [lax.ppermute(wide, axes, pairs) for pairs in plan.lon_pairs]

    near = {
        "count": edge_count,
        "wide": wide,
        "even_rows": even_rows,
        "odd_rows": odd_rows,
        "coarse_rows": coarse_rows,
        **{
            name: at[name]
            for name in (
                "w_edge_mid",
                "edge_part",
                "node_part",
                "sent",
                "received",
            )
        },
    }
    far = {
        "w_edge_out": w_edge_out,
        "node": node_feat,
        "gain_edge": row(gain_edge),
        "shift_edge": row(shift_edge),
        "edge": edge_feat,
        "w_node_in": w_node_in,
        "w_node_out": w_node_out,
        "gain_node": row(gain_node),
        "shift_node": row(shift_node),
        "cot_node": cot_node,
        "cot_edge": cot_edge,
    }
    copies = {name: (name, None) for name in far if name not in ("w_edge_in", "w_node_in")}
    copies["w_node_low"] = ("w_node_in", 1)
    copies["w_node_top"] = ("w_node_in", 0)
    plan.main_names, plan.main_copies, plan.main_held = [*near, *far], copies, list(copies)
    outs = [
        ((max(kept, SENT_ROWS), width), BF16),
        ((max(kept, SENT_ROWS), width), BF16),
        ((plan.coarse, width), F32),
        ((kept, width), F32),
        ((2 * nodes, width), BF16),
        ((edges, width), BF16),
        ((nodes, width), F32),
        (node_feat.shape, BF16),
    ]
    (
        even_grad,
        odd_grad,
        coarse_grad,
        kept_grad,
        agg_grad,
        edge_dpre,
        local,
        new_nodes,
    ) = call(
        with_plan(main_kernel),
        "main",
        outs,
        list(near.values()),
        far=list(far.values()),
        scratch=[VMEM((plan.table, width), BF16), VMEM(node_feat.shape, BF16)]
        + [
            VMEM(*(square if part is not None else (far[source].shape, far[source].dtype)))
            for source, part in copies.values()
        ]
        + [sems(len(copies) + 1)],
        flops=2 * 5 * edges * width * width,
        mib=20,
        results=1,
    )

    even_back, odd_back = [
        lax.ppermute(grad, axes, pairs)
        for grad, pairs in zip((even_grad, odd_grad), plan.lon_pairs)
    ]
    (coarse_send,) = call(
        with_plan(gather_kernel), "gather", [(coarse_shape, F32)], [coarse_grad, coarse_grad]
    )
    coarse_back = lax.all_to_all(coarse_send, axes, 0, 0, tiled=True)
    mine, *lat_sends = call(
        with_plan(middle_kernel),
        "middle",
        [((halo, width), F32)] + [((halo, width), BF16)] * len(plan.lat_pairs),
        [kept_grad, even_back, odd_back],
    )
    lat_back = [
        lax.ppermute(grad, axes, pairs) for grad, pairs in zip(lat_sends, plan.lat_pairs)
    ]
    grad_local, grad_edges = call(
        with_plan(behind_kernel),
        "behind",
        [((nodes, width), F32), (edge_feat.shape, BF16)],
        [at["received"], edge_dpre, agg_grad, local, mine],
        far=[w_edge_in, cot_edge],
        scratch=[VMEM(*square), VMEM(*square), *like([cot_edge, edge_feat]), sems(4)],
        flops=2 * (edges + nodes) * width * width,
        mib=8,
        results=1,
    )
    (grad_nodes,) = call(
        with_plan(last_kernel),
        "last",
        [(node_feat.shape, BF16)],
        [grad_local, mine, at["place"], at["at_coarse"], coarse_back, *lat_back],
        results=1,
    )
    return new_nodes, grad_nodes, grad_edges


def solution(mesh):
    lon, lat = mesh.shape["lon"], mesh.shape["lat"]
    cells = lambda rank: P("lon", "lat", *([None] * (rank - 2)))

    def sharded(*args):
        node_feat, edge_feat, halo_list, coarse_list = args[0], args[1], args[5], args[6]
        plan = Plan(
            lon,
            lat,
            node_feat.shape[2],
            edge_feat.shape[2],
            halo_list.shape[2],
            coarse_list.shape[2],
            node_feat.shape[3],
        )
        return body(plan, *args)

    ranks = (4, 4, 3, 3, 2, 3, 3)
    return jax.shard_map(
        sharded,
        mesh=mesh,
        in_specs=tuple(cells(r) for r in ranks) + (P(),) * 10 + (cells(4), cells(4)),
        out_specs=(cells(4), cells(4), cells(4)),
        check_vma=False,
    )
```

```python
import functools

import jax
import jax.numpy as jnp
from jax import lax
from jax.experimental import pallas as pl
from jax.experimental.pallas import tpu as pltpu
from jax.sharding import PartitionSpec as P

F32 = jnp.float32
BF16 = jnp.bfloat16
VMEM = pltpu.VMEM
SENT_ROWS = 128


def dot_nn(a, b):
    return jnp.dot(a, b, preferred_element_type=F32)


def dot_tn(a, b):
    return lax.dot_general(a, b, (((0,), (0,)), ((), ())), preferred_element_type=F32)


def dot_nt(a, b):
    return lax.dot_general(a, b, (((1,), (1,)), ((), ())), preferred_element_type=F32)


def as_one_hot(mask):
    return jnp.where(mask, 1.0, 0.0).astype(BF16)


def one_hot_rows(index_row, rows):
    return lax.broadcasted_iota(jnp.int32, (rows, index_row.shape[1]), 0) == index_row


def live_one_hot(index_row, rows, count):
    lanes = lax.broadcasted_iota(jnp.int32, (rows, index_row.shape[1]), 1)
    return as_one_hot(one_hot_rows(index_row, rows) & (lanes < count))


def in_two(values):
    head = values.astype(BF16)
    tail = (values - head.astype(F32)).astype(BF16)
    return jnp.concatenate([head, tail], axis=0)


def normed_rows(out_rows):
    centre = out_rows - jnp.mean(out_rows, axis=1, keepdims=True)
    inv_std = lax.rsqrt(jnp.mean(centre * centre, axis=1, keepdims=True) + 1e-05)
    return centre * inv_std, inv_std


def norm_backward(grad_norm, normed, inv_std):
    return inv_std * (
        grad_norm
        - jnp.mean(grad_norm, axis=1, keepdims=True)
        - normed * jnp.mean(grad_norm * normed, axis=1, keepdims=True)
    )


def silu_slope(pre, sig):
    return sig * (1.0 + pre * (1.0 - sig))


class Moves:
    def __init__(self, sems):
        self.sems, self.used = sems, 0

    def start(self, source, target):
        copy = pltpu.make_async_copy(source, target, self.sems.at[self.used])
        self.used += 1
        copy.start()
        return copy


class Plan:
    def __init__(self, lon, lat, nodes, edges, halo, owned, width):
        self.lon, self.lat = lon, lat
        self.nodes, self.edges, self.halo, self.owned, self.width = nodes, edges, halo, owned, width
        self.devices = lon * lat
        self.coarse = self.devices * owned
        flat = lambda i, j: (i % lon) * lat + j
        swap = lambda pairs: [p for a, b in pairs for p in ((a, b), (b, a))]
        lat_sets = [
            [(k, k + 1) for k in range(0, lat - 1, 2)],
            [(k, k + 1) for k in range(1, lat - 1, 2)],
        ]
        self.lat_pairs = [
            swap([(flat(i, a), flat(i, b)) for i in range(lon) for a, b in pairs])
            for pairs in lat_sets
            if pairs
        ]
        self.lon_pairs = [
            swap([(flat(i, j), flat(i + 1, j)) for i in range(first, lon, 2) for j in range(lat)])
            for first in (0, 1)
        ]
        self.per_lon = 1 + len(self.lat_pairs)
        self.blocks = 3 * self.per_lon
        self.table = nodes + self.blocks * halo + self.coarse

    def positions(self, sender):
        nodes, halo = self.nodes, self.halo
        lon_odd = lax.rem(lax.axis_index("lon"), 2)
        lat_odd = lax.rem(lax.axis_index("lat"), 2)
        lon_step = [1, 2 - 2 * lon_odd, 2 * lon_odd]
        lat_step = [1, 2 - 2 * lat_odd, 2 * lat_odd][: self.per_lon]
        past = sender - (nodes + 9 * halo)
        if self.owned > 1:
            past = jnp.where(
                past >= 0, lax.rem(past, self.owned) * self.devices + past // self.owned, past
            )
        found = jnp.where(past >= 0, past + (nodes + self.blocks * halo), sender)
        place = 0
        for a in lon_step:
            for b in lat_step:
                row = sender - (nodes + (3 * a + b) * halo)
                inside = (row >= 0) & (row < halo) & (sender >= nodes)
                found = jnp.where(inside, row + (nodes + place * halo), found)
                place += 1
        return found


def pack_kernel(plan, node, halo_list, coarse_list, border, coarse, node_s, halo_s, list_s, sems):
    moves = Moves(sems)
    pairs = ((coarse_list, list_s), (halo_list, halo_s), (node, node_s))
    for copy in [moves.start(*pair) for pair in pairs]:
        copy.wait()
    rows = node_s[0, 0]
    pick = as_one_hot(one_hot_rows(halo_s[0], plan.nodes))
    border[: plan.halo] = dot_tn(pick, rows).astype(BF16)
    own = dot_tn(as_one_hot(one_hot_rows(list_s[0], plan.nodes)), rows)
    parts = plan.width // 128
    pieces = [
        own[k : k + 1, q * 128 : (q + 1) * 128] for k in range(plan.owned) for q in range(parts)
    ]
    coarse[...] = jnp.broadcast_to(jnp.concatenate(pieces, axis=0)[None], coarse.shape)


def block_of(ref, part, width):
    return ref if part is None else ref.at[pl.ds(part * width, width)]


def ahead_kernel(plan, *refs):
    operands = dict(zip(plan.ahead_in, refs))
    refs = refs[len(plan.ahead_in) :]
    held = dict(zip(plan.ahead_out, refs))
    sems = refs[-1]
    held.update(zip(plan.ahead_held, refs[len(plan.ahead_out) : -1]))
    moves = Moves(sems)
    width, nodes = plan.width, plan.nodes
    copies = {
        name: moves.start(block_of(operands[source], part, width), held[name])
        for name, (source, part) in plan.ahead_copies.items()
    }

    def got(name):
        if name in copies:
            copies.pop(name).wait()
        return held[name]

    count = got("count")[...]
    received = live_one_hot(got("receivers")[0], nodes, count)
    held["received"][...] = received
    held["sent"][...] = as_one_hot(
        one_hot_rows(plan.positions(got("senders")[0]), plan.table)
    )
    place = as_one_hot(one_hot_rows(got("halo_list")[0], nodes))
    held["place"][...] = jnp.concatenate([place, place], axis=1)
    at_coarse = one_hot_rows(got("coarse_list")[0], nodes)
    held["at_coarse"][...] = jnp.where(at_coarse, 1.0, 0.0).astype(F32)
    rows = got("node")[0, 0]
    at_receiver = dot_tn(received, rows).astype(BF16)
    held["edge_part"][...] = (
        dot_nn(got("edge")[0, 0], got("w_edge_top")[...])
        + dot_nn(at_receiver, got("w_edge_low")[...])
        + got("b_edge_in")[...]
    )
    held["node_part"][...] = dot_nn(rows, got("w_node_top")[...]) + got("b_node_in")[...]
    for copy in copies.values():
        copy.wait()


def join_kernel(plan, *refs):
    for k, part in enumerate(refs[:-1]):
        refs[-1][k * plan.halo : (k + 1) * plan.halo] = part[: plan.halo]


def edge_cotangent(cot_edge, received, agg_grad):
    twice = jnp.concatenate([received, received], axis=0)
    return cot_edge[0, 0].astype(F32) + dot_tn(twice, agg_grad)


def main_kernel(plan, *refs):
    here = dict(zip(plan.main_names, refs))
    refs = refs[len(plan.main_names) :]
    even_grad, odd_grad, kept_grad, agg_out, edge_dpre_out, local = refs[:6]
    new_nodes, coarse_grad, table, new_s, tiles, coarse_s = refs[6:12]
    sems, held = refs[-1], dict(zip(plan.main_held, refs[12:-1]))
    nodes, halo, width = plan.nodes, plan.halo, plan.width
    sent, received = here["sent"], here["received"][...]
    live = jnp.where(
        lax.broadcasted_iota(jnp.int32, (plan.edges, 1), 0) < here["count"][0, 0], 1.0, 0.0
    ).astype(F32)
    moves = Moves(sems)
    copies = {
        name: moves.start(block_of(here[source], part, width), held[name])
        for name, (source, part) in plan.main_copies.items()
    }

    def got(name):
        if name in copies:
            copies.pop(name).wait()
        return held[name] if name in held else here[name]

    start = nodes
    table[:nodes] = got("node")[0, 0]
    for name in ("wide", "even_rows", "odd_rows"):
        rim = plan.per_lon * halo
        table[start : start + rim] = got(name)[:rim]
        start += rim
    parts = width // 128
    for k in range(plan.owned):
        for q in range(parts):
            table[start : start + plan.devices, q * 128 : (q + 1) * 128] = got("coarse_rows")[
                :, k * parts + q, :
            ].astype(BF16)
        start += plan.devices

    w_edge_mid = got("w_edge_mid")[...]
    at_sender = dot_tn(sent[...], table[...]).astype(BF16)
    edge_pre = got("edge_part")[...] + dot_nn(at_sender, w_edge_mid)
    edge_sig = jax.nn.sigmoid(edge_pre)
    edge_out = dot_nn((edge_pre * edge_sig).astype(BF16), got("w_edge_out")[...])
    edge_normed, edge_rstd = normed_rows(edge_out)
    edge_upd = edge_normed * got("gain_edge")[...] + got("shift_edge")[...]
    new_edge = (got("edge")[0, 0].astype(F32) + live * edge_upd).astype(BF16)
    aggregated = dot_nn(received, new_edge).astype(BF16)

    node_pre = got("node_part")[...] + dot_nn(aggregated, got("w_node_low")[...])
    node_sig = jax.nn.sigmoid(node_pre)
    node_out = dot_nn((node_pre * node_sig).astype(BF16), got("w_node_out")[...])
    node_normed, node_rstd = normed_rows(node_out)
    node_upd = node_normed * got("gain_node")[...] + got("shift_node")[...]
    new_s[0, 0] = (got("node")[0, 0].astype(F32) + node_upd).astype(BF16)
    leaving = moves.start(new_s, new_nodes)

    node_dout = norm_backward(
        got("cot_node")[0, 0].astype(F32) * got("gain_node")[...], node_normed, node_rstd
    ).astype(BF16)
    node_dpre = (
        dot_nt(node_dout, got("w_node_out")[...]) * silu_slope(node_pre, node_sig)
    ).astype(BF16)
    agg_grad = in_two(dot_nt(node_dpre, got("w_node_low")[...]))
    agg_out[...] = agg_grad
    edge_cot = edge_cotangent(got("cot_edge"), received, agg_grad)

    edge_dout = norm_backward(
        live * edge_cot * got("gain_edge")[...], edge_normed, edge_rstd
    ).astype(BF16)
    edge_dpre = (
        dot_nt(edge_dout, got("w_edge_out")[...]) * silu_slope(edge_pre, edge_sig)
    ).astype(BF16)
    edge_dpre_out[...] = edge_dpre
    away_grad = dot_nt(dot_nn(sent[...], edge_dpre).astype(BF16), w_edge_mid)
    own_grad, away_grad = away_grad[:nodes], away_grad[nodes:]
    kept = plan.per_lon * halo
    start = 3 * kept
    for k in range(plan.owned):
        for q in range(parts):
            tiles[:, k * parts + q, :] = away_grad[
                start : start + plan.devices, q * 128 : (q + 1) * 128
            ]
        start += plan.devices
    coarse_s[...] = tiles[...].astype(BF16)
    coarse_leaving = moves.start(coarse_s, coarse_grad)
    even_grad[...] = away_grad[kept : 2 * kept].astype(BF16)
    odd_grad[...] = away_grad[2 * kept : 3 * kept].astype(BF16)
    kept_grad[...] = away_grad[:kept]
    local[...] = (
        got("cot_node")[0, 0].astype(F32) + dot_nt(node_dpre, got("w_node_top")[...]) + own_grad
    )
    leaving.wait()
    coarse_leaving.wait()


def behind_kernel(plan, *refs):
    received, edge_dpre, agg_grad, local, _, w_edge_in, cot_edge, grad_local, grad_edges = refs[:9]
    w_top_s, w_low_s, cot_s, grad_s, sems = refs[9:]
    moves, width = Moves(sems), plan.width
    top = moves.start(block_of(w_edge_in, 0, width), w_top_s)
    cot = moves.start(cot_edge, cot_s)
    low = moves.start(block_of(w_edge_in, 2, width), w_low_s)
    dpre = edge_dpre[...]
    at_receiver = dot_nn(received[...], dpre).astype(BF16)
    cot.wait()
    edge_cot = edge_cotangent(cot_s, received[...], agg_grad[...])
    top.wait()
    grad_s[0, 0] = (edge_cot + dot_nt(dpre, w_top_s[...])).astype(BF16)
    leaving = moves.start(grad_s, grad_edges)
    low.wait()
    grad_local[...] = local[...] + dot_nt(at_receiver, w_low_s[...])
    leaving.wait()


def middle_kernel(plan, kept, even, odd, mine, *lat_sends):
    total = kept[...] + even[...].astype(F32) + odd[...].astype(F32)
    mine[...] = total[: plan.halo]
    for k, out in enumerate(lat_sends):
        out[...] = total[(k + 1) * plan.halo : (k + 2) * plan.halo].astype(BF16)


def last_kernel(plan, *refs):
    grad_local, mine, place, at_coarse, coarse = refs[:5]
    out = refs[-1]
    total = mine[...]
    for part in refs[5:-1]:
        total = total + part[...].astype(F32)
    result = grad_local[...] + dot_nn(place[...], in_two(total))
    share = jnp.sum(coarse[...].astype(F32), axis=0)
    parts = plan.width // 128
    for k in range(plan.owned):
        row = jnp.concatenate([share[k * parts + q : k * parts + q + 1] for q in range(parts)], axis=1)
        result = result + at_coarse[:, k : k + 1] * row
    out[0, 0] = result.astype(BF16)


def call(body, name, outs, operands, far=(), scratch=(), flops=0, mib=4, results=0):
    whole = pl.BlockSpec(memory_space=VMEM)
    scalars = pl.BlockSpec(memory_space=pltpu.SMEM)
    anywhere = pl.BlockSpec(memory_space=pl.ANY)
    far = [pltpu.with_memory_space_constraint(a, pltpu.HBM) if a.size > 1 else a for a in far]
    moved = sum(a.size * a.dtype.itemsize for a in (*operands, *far))
    near = len(outs) - results
    return pl.pallas_call(
        body,
        name=name,
        out_shape=[VMEM(shape, dtype) for shape, dtype in outs[:near]]
        + [jax.ShapeDtypeStruct(shape, dtype) for shape, dtype in outs[near:]],
        in_specs=[scalars if a.size == 1 else whole for a in operands] + [anywhere] * len(far),
        out_specs=[whole] * near + [anywhere if scratch else whole] * results,
        scratch_shapes=list(scratch),
        compiler_params=pltpu.CompilerParams(vmem_limit_bytes=mib * 1024 * 1024),
        cost_estimate=pl.CostEstimate(flops=flops, bytes_accessed=moved, transcendentals=0),
    )(*operands, *far)


def like(arrays):
    return [VMEM(a.shape, a.dtype) for a in arrays]


def sems(count):
    return pltpu.SemaphoreType.DMA((count,))


def body(
    plan,
    node_feat,
    edge_feat,
    senders,
    receivers,
    edge_count,
    halo_list,
    coarse_list,
    w_edge_in,
    b_edge_in,
    w_edge_out,
    gain_edge,
    shift_edge,
    w_node_in,
    b_node_in,
    w_node_out,
    gain_node,
    shift_node,
    cot_node,
    cot_edge,
):
    axes = ("lon", "lat")
    halo, width, nodes, edges = plan.halo, plan.width, plan.nodes, plan.edges
    row = lambda vec: vec.reshape(1, width)
    with_plan = lambda kernel: functools.partial(kernel, plan)
    coarse_shape = (plan.devices, plan.owned * width // 128, 128)
    kept = plan.per_lon * halo

    operands = [node_feat, halo_list, coarse_list]
    border, coarse_out = call(
        with_plan(pack_kernel),
        "pack",
        [((max(halo, SENT_ROWS), width), BF16), (coarse_shape, F32)],
        [],
        far=operands,
        scratch=like(operands) + [sems(3)],
    )
    coarse_rows = lax.all_to_all(coarse_out, axes, 0, 0, tiled=True)
    lat_rows = [lax.ppermute(border, axes, pairs) for pairs in plan.lat_pairs]

    far = {
        "count": edge_count,
        "receivers": receivers,
        "node": node_feat,
        "edge": edge_feat,
        "w_edge_in": w_edge_in,
        "b_edge_in": row(b_edge_in),
        "senders": senders,
        "halo_list": halo_list,
        "coarse_list": coarse_list,
        "w_node_in": w_node_in,
        "b_node_in": row(b_node_in),
        "w_edge_out": w_edge_out,
        "gain_edge": row(gain_edge),
        "shift_edge": row(shift_edge),
        "gain_node": row(gain_node),
        "shift_node": row(shift_node),
    }
    square = ((width, width), BF16)
    copies = {name: (name, None) for name in far if name not in ("w_edge_in", "w_node_in")}
    copies["w_edge_top"] = ("w_edge_in", 0)
    copies["w_edge_low"] = ("w_edge_in", 2)
    copies["w_node_top"] = ("w_node_in", 0)
    copies["w_edge_mid"] = ("w_edge_in", 1)
    passed_on = ("node", "w_edge_out", "gain_edge", "shift_edge", "gain_node", "shift_node")
    outs = {
        **{name: (far[name].shape, far[name].dtype) for name in passed_on},
        "w_edge_mid": square,
        "edge_part": ((edges, width), F32),
        "node_part": ((nodes, width), F32),
        "sent": ((plan.table, edges), BF16),
        "received": ((nodes, edges), BF16),
        "place": ((nodes, 2 * halo), BF16),
        "at_coarse": ((nodes, plan.owned), F32),
    }
    held = {
        name: square if part is not None else (far[source].shape, far[source].dtype)
        for name, (source, part) in copies.items()
        if name not in outs
    }
    plan.ahead_in, plan.ahead_out, plan.ahead_held = list(far), list(outs), list(held)
    plan.ahead_copies = copies
    at = dict(
        zip(
            outs,
            call(
                with_plan(ahead_kernel),
                "ahead",
                list(outs.values()),
                [],
                far=list(far.values()),
                scratch=[VMEM(*kind) for kind in held.values()] + [sems(len(copies))],
                flops=2 * (2 * edges + nodes) * width * width,
                mib=12,
            ),
        )
    )

    (wide,) = call(with_plan(join_kernel), "join", [((kept, width), BF16)], [border, *lat_rows])
    even_rows, odd_rows = [lax.ppermute(wide, axes, pairs) for pairs in plan.lon_pairs]

    near = {
        "count": edge_count,
        "wide": wide,
        "even_rows": even_rows,
        "odd_rows": odd_rows,
        "coarse_rows": coarse_rows,
        **{
            name: at[name]
            for name in (
                "w_edge_mid",
                "edge_part",
                "node_part",
                "sent",
                "received",
                *passed_on,
            )
        },
    }
    far = {
        "edge": edge_feat,
        "w_node_in": w_node_in,
        "w_node_out": w_node_out,
        "cot_node": cot_node,
        "cot_edge": cot_edge,
    }
    copies = {
        "edge": ("edge", None),
        "w_node_low": ("w_node_in", 1),
        "w_node_out": ("w_node_out", None),
        "cot_node": ("cot_node", None),
        "cot_edge": ("cot_edge", None),
        "w_node_top": ("w_node_in", 0),
    }
    plan.main_names, plan.main_copies, plan.main_held = [*near, *far], copies, list(copies)
    outs = [
        ((kept, width), BF16),
        ((kept, width), BF16),
        ((kept, width), F32),
        ((2 * nodes, width), BF16),
        ((edges, width), BF16),
        ((nodes, width), F32),
        (node_feat.shape, BF16),
        (coarse_shape, BF16),
    ]
    (
        even_grad,
        odd_grad,
        kept_grad,
        agg_grad,
        edge_dpre,
        local,
        new_nodes,
        coarse_send,
    ) = call(
        with_plan(main_kernel),
        "main",
        outs,
        list(near.values()),
        far=list(far.values()),
        scratch=[VMEM((plan.table, width), BF16), VMEM(node_feat.shape, BF16)]
        + [VMEM(coarse_shape, F32), VMEM(coarse_shape, BF16)]
        + [
            VMEM(*(square if part is not None else (far[source].shape, far[source].dtype)))
            for source, part in copies.values()
        ]
        + [sems(len(copies) + 2)],
        flops=2 * 5 * edges * width * width,
        mib=20,
        results=2,
    )

    even_back, odd_back = [
        lax.ppermute(grad, axes, pairs)
        for grad, pairs in zip((even_grad, odd_grad), plan.lon_pairs)
    ]
    coarse_back = lax.all_to_all(coarse_send, axes, 0, 0, tiled=True)
    mine, *lat_sends = call(
        with_plan(middle_kernel),
        "middle",
        [((halo, width), F32)] + [((halo, width), BF16)] * len(plan.lat_pairs),
        [kept_grad, even_back, odd_back],
    )
    lat_back = [
        lax.ppermute(grad, axes, pairs) for grad, pairs in zip(lat_sends, plan.lat_pairs)
    ]
    grad_local, grad_edges = call(
        with_plan(behind_kernel),
        "behind",
        [((nodes, width), F32), (edge_feat.shape, BF16)],
        [at["received"], edge_dpre, agg_grad, local, mine],
        far=[w_edge_in, cot_edge],
        scratch=[VMEM(*square), VMEM(*square), *like([cot_edge, edge_feat]), sems(4)],
        flops=2 * (edges + nodes) * width * width,
        mib=8,
        results=1,
    )
    (grad_nodes,) = call(
        with_plan(last_kernel),
        "last",
        [(node_feat.shape, BF16)],
        [grad_local, mine, at["place"], at["at_coarse"], coarse_back, *lat_back],
        results=1,
    )
    return new_nodes, grad_nodes, grad_edges


def solution(mesh):
    lon, lat = mesh.shape["lon"], mesh.shape["lat"]
    cells = lambda rank: P("lon", "lat", *([None] * (rank - 2)))

    def sharded(*args):
        node_feat, edge_feat, halo_list, coarse_list = args[0], args[1], args[5], args[6]
        plan = Plan(
            lon,
            lat,
            node_feat.shape[2],
            edge_feat.shape[2],
            halo_list.shape[2],
            coarse_list.shape[2],
            node_feat.shape[3],
        )
        return body(plan, *args)

    ranks = (4, 4, 3, 3, 2, 3, 3)
    return jax.shard_map(
        sharded,
        mesh=mesh,
        in_specs=tuple(cells(r) for r in ranks) + (P(),) * 10 + (cells(4), cells(4)),
        out_specs=(cells(4), cells(4), cells(4)),
        check_vma=False,
    )
```

```python
import functools

import jax
import jax.numpy as jnp
from jax import lax
from jax.experimental import pallas as pl
from jax.experimental.pallas import tpu as pltpu
from jax.sharding import PartitionSpec as P

F32 = jnp.float32
BF16 = jnp.bfloat16
VMEM = pltpu.VMEM
SENT_ROWS = 128


def dot_nn(a, b):
    return jnp.dot(a, b, preferred_element_type=F32)


def dot_tn(a, b):
    return lax.dot_general(a, b, (((0,), (0,)), ((), ())), preferred_element_type=F32)


def dot_nt(a, b):
    return lax.dot_general(a, b, (((1,), (1,)), ((), ())), preferred_element_type=F32)


def as_one_hot(mask):
    return jnp.where(mask, 1.0, 0.0).astype(BF16)


def one_hot_rows(index_row, rows):
    return lax.broadcasted_iota(jnp.int32, (rows, index_row.shape[1]), 0) == index_row


def live_one_hot(index_row, rows, count):
    lanes = lax.broadcasted_iota(jnp.int32, (rows, index_row.shape[1]), 1)
    return as_one_hot(one_hot_rows(index_row, rows) & (lanes < count))


def in_two(values):
    head = values.astype(BF16)
    tail = (values - head.astype(F32)).astype(BF16)
    return jnp.concatenate([head, tail], axis=0)


def normed_rows(out_rows):
    centre = out_rows - jnp.mean(out_rows, axis=1, keepdims=True)
    inv_std = lax.rsqrt(jnp.mean(centre * centre, axis=1, keepdims=True) + 1e-05)
    return centre * inv_std, inv_std


def norm_backward(grad_norm, normed, inv_std):
    return inv_std * (
        grad_norm
        - jnp.mean(grad_norm, axis=1, keepdims=True)
        - normed * jnp.mean(grad_norm * normed, axis=1, keepdims=True)
    )


def silu_slope(pre, sig):
    return sig * (1.0 + pre * (1.0 - sig))


class Moves:
    def __init__(self, sems):
        self.sems, self.used = sems, 0

    def start(self, source, target):
        copy = pltpu.make_async_copy(source, target, self.sems.at[self.used])
        self.used += 1
        copy.start()
        return copy


class Plan:
    def __init__(self, lon, lat, nodes, edges, halo, owned, width):
        self.lon, self.lat = lon, lat
        self.nodes, self.edges, self.halo, self.owned, self.width = nodes, edges, halo, owned, width
        self.devices = lon * lat
        self.coarse = self.devices * owned
        flat = lambda i, j: (i % lon) * lat + j
        swap = lambda pairs: [p for a, b in pairs for p in ((a, b), (b, a))]
        lat_sets = [
            [(k, k + 1) for k in range(0, lat - 1, 2)],
            [(k, k + 1) for k in range(1, lat - 1, 2)],
        ]
        self.lat_pairs = [
            swap([(flat(i, a), flat(i, b)) for i in range(lon) for a, b in pairs])
            for pairs in lat_sets
            if pairs
        ]
        self.lon_pairs = [
            swap([(flat(i, j), flat(i + 1, j)) for i in range(first, lon, 2) for j in range(lat)])
            for first in (0, 1)
        ]
        self.per_lon = 1 + len(self.lat_pairs)
        self.blocks = 3 * self.per_lon
        self.table = nodes + self.blocks * halo + self.coarse

    def positions(self, sender):
        nodes, halo = self.nodes, self.halo
        lon_odd = lax.rem(lax.axis_index("lon"), 2)
        lat_odd = lax.rem(lax.axis_index("lat"), 2)
        lon_step = [1, 2 - 2 * lon_odd, 2 * lon_odd]
        lat_step = [1, 2 - 2 * lat_odd, 2 * lat_odd][: self.per_lon]
        past = sender - (nodes + 9 * halo)
        if self.owned > 1:
            past = jnp.where(
                past >= 0, lax.rem(past, self.owned) * self.devices + past // self.owned, past
            )
        found = jnp.where(past >= 0, past + (nodes + self.blocks * halo), sender)
        place = 0
        for a in lon_step:
            for b in lat_step:
                row = sender - (nodes + (3 * a + b) * halo)
                inside = (row >= 0) & (row < halo) & (sender >= nodes)
                found = jnp.where(inside, row + (nodes + place * halo), found)
                place += 1
        return found


def pack_kernel(plan, node, halo_list, coarse_list, border, coarse, node_s, halo_s, list_s, sems):
    moves = Moves(sems)
    pairs = ((coarse_list, list_s), (halo_list, halo_s), (node, node_s))
    for copy in [moves.start(*pair) for pair in pairs]:
        copy.wait()
    rows = node_s[0, 0]
    pick = as_one_hot(one_hot_rows(halo_s[0], plan.nodes))
    border[: plan.halo] = dot_tn(pick, rows).astype(BF16)
    own = dot_tn(as_one_hot(one_hot_rows(list_s[0], plan.nodes)), rows)
    parts = plan.width // 128
    pieces = [
        own[k : k + 1, q * 128 : (q + 1) * 128] for k in range(plan.owned) for q in range(parts)
    ]
    coarse[...] = jnp.broadcast_to(jnp.concatenate(pieces, axis=0)[None], coarse.shape)


def block_of(ref, part, width):
    return ref if part is None else ref.at[pl.ds(part * width, width)]


def ahead_kernel(plan, *refs):
    operands = dict(zip(plan.ahead_in, refs))
    refs = refs[len(plan.ahead_in) :]
    held = dict(zip(plan.ahead_out, refs))
    sems = refs[-1]
    held.update(zip(plan.ahead_held, refs[len(plan.ahead_out) : -1]))
    moves = Moves(sems)
    width, nodes = plan.width, plan.nodes
    copies = {
        name: moves.start(block_of(operands[source], part, width), held[name])
        for name, (source, part) in plan.ahead_copies.items()
    }

    def got(name):
        if name in copies:
            copies.pop(name).wait()
        return held[name]

    count = got("count")[...]
    received = live_one_hot(got("receivers")[0], nodes, count)
    held["received"][...] = received
    held["sent"][...] = as_one_hot(
        one_hot_rows(plan.positions(got("senders")[0]), plan.table)
    )
    place = as_one_hot(one_hot_rows(got("halo_list")[0], nodes))
    held["place"][...] = jnp.concatenate([place, place], axis=1)
    at_coarse = one_hot_rows(got("coarse_list")[0], nodes)
    held["at_coarse"][...] = jnp.where(at_coarse, 1.0, 0.0).astype(F32)
    rows = got("node")[0, 0]
    at_receiver = dot_tn(received, rows).astype(BF16)
    held["edge_part"][...] = (
        dot_nn(got("edge")[0, 0], got("w_edge_top")[...])
        + dot_nn(at_receiver, got("w_edge_low")[...])
        + got("b_edge_in")[...]
    )
    held["node_part"][...] = dot_nn(rows, got("w_node_top")[...]) + got("b_node_in")[...]
    for copy in copies.values():
        copy.wait()


def join_kernel(plan, *refs):
    for k, part in enumerate(refs[:-1]):
        refs[-1][k * plan.halo : (k + 1) * plan.halo] = part[: plan.halo]


def edge_cotangent(cot_edge, received, agg_grad):
    twice = jnp.concatenate([received, received], axis=0)
    return cot_edge[0, 0].astype(F32) + dot_tn(twice, agg_grad)


def main_kernel(plan, *refs):
    here = dict(zip(plan.main_names, refs))
    refs = refs[len(plan.main_names) :]
    kept_grad, agg_out, edge_dpre_out, local = refs[:4]
    lat_grads, refs = refs[4 : 3 + plan.per_lon], refs[3 + plan.per_lon :]
    new_nodes, coarse_grad, table, new_s, tiles, coarse_s = refs[:6]
    sems, held = refs[-1], dict(zip(plan.main_held, refs[6:-1]))
    nodes, halo, width = plan.nodes, plan.halo, plan.width
    sent, received = here["sent"], here["received"][...]
    live = jnp.where(
        lax.broadcasted_iota(jnp.int32, (plan.edges, 1), 0) < here["count"][0, 0], 1.0, 0.0
    ).astype(F32)
    moves = Moves(sems)
    copies = {
        name: moves.start(block_of(here[source], part, width), held[name])
        for name, (source, part) in plan.main_copies.items()
    }

    def got(name):
        if name in copies:
            copies.pop(name).wait()
        return held[name] if name in held else here[name]

    start = nodes
    table[:nodes] = got("node")[0, 0]
    for name in ("wide", "even_rows", "odd_rows"):
        rim = plan.per_lon * halo
        table[start : start + rim] = got(name)[:rim]
        start += rim
    parts = width // 128
    for k in range(plan.owned):
        for q in range(parts):
            table[start : start + plan.devices, q * 128 : (q + 1) * 128] = got("coarse_rows")[
                :, k * parts + q, :
            ].astype(BF16)
        start += plan.devices

    w_edge_mid = got("w_edge_mid")[...]
    at_sender = dot_tn(sent[...], table[...]).astype(BF16)
    edge_pre = got("edge_part")[...] + dot_nn(at_sender, w_edge_mid)
    edge_sig = jax.nn.sigmoid(edge_pre)
    edge_out = dot_nn((edge_pre * edge_sig).astype(BF16), got("w_edge_out")[...])
    edge_normed, edge_rstd = normed_rows(edge_out)
    edge_upd = edge_normed * got("gain_edge")[...] + got("shift_edge")[...]
    new_edge = (got("edge")[0, 0].astype(F32) + live * edge_upd).astype(BF16)
    aggregated = dot_nn(received, new_edge).astype(BF16)

    node_pre = got("node_part")[...] + dot_nn(aggregated, got("w_node_low")[...])
    node_sig = jax.nn.sigmoid(node_pre)
    node_out = dot_nn((node_pre * node_sig).astype(BF16), got("w_node_out")[...])
    node_normed, node_rstd = normed_rows(node_out)
    node_upd = node_normed * got("gain_node")[...] + got("shift_node")[...]
    new_s[0, 0] = (got("node")[0, 0].astype(F32) + node_upd).astype(BF16)
    leaving = moves.start(new_s, new_nodes)

    node_dout = norm_backward(
        got("cot_node")[0, 0].astype(F32) * got("gain_node")[...], node_normed, node_rstd
    ).astype(BF16)
    node_dpre = (
        dot_nt(node_dout, got("w_node_out")[...]) * silu_slope(node_pre, node_sig)
    ).astype(BF16)
    agg_grad = in_two(dot_nt(node_dpre, got("w_node_low")[...]))
    agg_out[...] = agg_grad
    edge_cot = edge_cotangent(got("cot_edge"), received, agg_grad)

    edge_dout = norm_backward(
        live * edge_cot * got("gain_edge")[...], edge_normed, edge_rstd
    ).astype(BF16)
    edge_dpre = (
        dot_nt(edge_dout, got("w_edge_out")[...]) * silu_slope(edge_pre, edge_sig)
    ).astype(BF16)
    edge_dpre_out[...] = edge_dpre
    away_grad = dot_nt(dot_nn(sent[...], edge_dpre).astype(BF16), w_edge_mid)
    own_grad, away_grad = away_grad[:nodes], away_grad[nodes:]
    kept = plan.per_lon * halo
    start = 3 * kept
    for k in range(plan.owned):
        for q in range(parts):
            tiles[:, k * parts + q, :] = away_grad[
                start : start + plan.devices, q * 128 : (q + 1) * 128
            ]
        start += plan.devices
    coarse_s[...] = tiles[...].astype(BF16)
    coarse_leaving = moves.start(coarse_s, coarse_grad)
    for a in range(3):
        rows = slice(a * halo, (a + 1) * halo)
        kept_grad[rows] = away_grad[a * kept : a * kept + halo].astype(BF16)
        for k, lat_grad in enumerate(lat_grads):
            first = a * kept + (k + 1) * halo
            lat_grad[rows] = away_grad[first : first + halo].astype(BF16)
    local[...] = (
        got("cot_node")[0, 0].astype(F32) + dot_nt(node_dpre, got("w_node_top")[...]) + own_grad
    )
    leaving.wait()
    coarse_leaving.wait()


def behind_kernel(plan, *refs):
    received, edge_dpre, agg_grad, local, _, w_edge_in, cot_edge, grad_local, grad_edges = refs[:9]
    w_top_s, w_low_s, cot_s, grad_s, sems = refs[9:]
    moves, width = Moves(sems), plan.width
    top = moves.start(block_of(w_edge_in, 0, width), w_top_s)
    cot = moves.start(cot_edge, cot_s)
    low = moves.start(block_of(w_edge_in, 2, width), w_low_s)
    dpre = edge_dpre[...]
    at_receiver = dot_nn(received[...], dpre).astype(BF16)
    cot.wait()
    edge_cot = edge_cotangent(cot_s, received[...], agg_grad[...])
    top.wait()
    grad_s[0, 0] = (edge_cot + dot_nt(dpre, w_top_s[...])).astype(BF16)
    leaving = moves.start(grad_s, grad_edges)
    low.wait()
    grad_local[...] = local[...] + dot_nt(at_receiver, w_low_s[...])
    leaving.wait()


def middle_kernel(plan, kept, *refs):
    total = kept[...].astype(F32)
    for part in refs[:-3]:
        total = total + part[...].astype(F32)
    mine, even, odd = refs[-3:]
    halo = plan.halo
    mine[...] = total[:halo]
    even[...] = total[halo : 2 * halo].astype(BF16)
    odd[...] = total[2 * halo :].astype(BF16)


def last_kernel(plan, *refs):
    grad_local, mine, place, at_coarse, coarse = refs[:5]
    out = refs[-1]
    total = mine[...]
    for part in refs[5:-1]:
        total = total + part[...].astype(F32)
    result = grad_local[...] + dot_nn(place[...], in_two(total))
    share = jnp.sum(coarse[...].astype(F32), axis=0)
    parts = plan.width // 128
    for k in range(plan.owned):
        row = jnp.concatenate([share[k * parts + q : k * parts + q + 1] for q in range(parts)], axis=1)
        result = result + at_coarse[:, k : k + 1] * row
    out[0, 0] = result.astype(BF16)


def call(body, name, outs, operands, far=(), scratch=(), flops=0, mib=4, results=0):
    whole = pl.BlockSpec(memory_space=VMEM)
    scalars = pl.BlockSpec(memory_space=pltpu.SMEM)
    anywhere = pl.BlockSpec(memory_space=pl.ANY)
    far = [pltpu.with_memory_space_constraint(a, pltpu.HBM) if a.size > 1 else a for a in far]
    moved = sum(a.size * a.dtype.itemsize for a in (*operands, *far))
    near = len(outs) - results
    return pl.pallas_call(
        body,
        name=name,
        out_shape=[VMEM(shape, dtype) for shape, dtype in outs[:near]]
        + [jax.ShapeDtypeStruct(shape, dtype) for shape, dtype in outs[near:]],
        in_specs=[scalars if a.size == 1 else whole for a in operands] + [anywhere] * len(far),
        out_specs=[whole] * near + [anywhere if scratch else whole] * results,
        scratch_shapes=list(scratch),
        compiler_params=pltpu.CompilerParams(vmem_limit_bytes=mib * 1024 * 1024),
        cost_estimate=pl.CostEstimate(flops=flops, bytes_accessed=moved, transcendentals=0),
    )(*operands, *far)


def like(arrays):
    return [VMEM(a.shape, a.dtype) for a in arrays]


def sems(count):
    return pltpu.SemaphoreType.DMA((count,))


def body(
    plan,
    node_feat,
    edge_feat,
    senders,
    receivers,
    edge_count,
    halo_list,
    coarse_list,
    w_edge_in,
    b_edge_in,
    w_edge_out,
    gain_edge,
    shift_edge,
    w_node_in,
    b_node_in,
    w_node_out,
    gain_node,
    shift_node,
    cot_node,
    cot_edge,
):
    axes = ("lon", "lat")
    halo, width, nodes, edges = plan.halo, plan.width, plan.nodes, plan.edges
    row = lambda vec: vec.reshape(1, width)
    with_plan = lambda kernel: functools.partial(kernel, plan)
    coarse_shape = (plan.devices, plan.owned * width // 128, 128)
    kept = plan.per_lon * halo

    operands = [node_feat, halo_list, coarse_list]
    border, coarse_out = call(
        with_plan(pack_kernel),
        "pack",
        [((max(halo, SENT_ROWS), width), BF16), (coarse_shape, F32)],
        [],
        far=operands,
        scratch=like(operands) + [sems(3)],
    )
    coarse_rows = lax.all_to_all(coarse_out, axes, 0, 0, tiled=True)
    lat_rows = [lax.ppermute(border, axes, pairs) for pairs in plan.lat_pairs]

    far = {
        "count": edge_count,
        "receivers": receivers,
        "node": node_feat,
        "edge": edge_feat,
        "w_edge_in": w_edge_in,
        "b_edge_in": row(b_edge_in),
        "senders": senders,
        "halo_list": halo_list,
        "coarse_list": coarse_list,
        "w_node_in": w_node_in,
        "b_node_in": row(b_node_in),
        "w_edge_out": w_edge_out,
        "gain_edge": row(gain_edge),
        "shift_edge": row(shift_edge),
        "gain_node": row(gain_node),
        "shift_node": row(shift_node),
    }
    square = ((width, width), BF16)
    copies = {name: (name, None) for name in far if name not in ("w_edge_in", "w_node_in")}
    copies["w_edge_top"] = ("w_edge_in", 0)
    copies["w_edge_low"] = ("w_edge_in", 2)
    copies["w_node_top"] = ("w_node_in", 0)
    copies["w_edge_mid"] = ("w_edge_in", 1)
    passed_on = ("node", "w_edge_out", "gain_edge", "shift_edge", "gain_node", "shift_node")
    outs = {
        **{name: (far[name].shape, far[name].dtype) for name in passed_on},
        "w_edge_mid": square,
        "edge_part": ((edges, width), F32),
        "node_part": ((nodes, width), F32),
        "sent": ((plan.table, edges), BF16),
        "received": ((nodes, edges), BF16),
        "place": ((nodes, 2 * halo), BF16),
        "at_coarse": ((nodes, plan.owned), F32),
    }
    held = {
        name: square if part is not None else (far[source].shape, far[source].dtype)
        for name, (source, part) in copies.items()
        if name not in outs
    }
    plan.ahead_in, plan.ahead_out, plan.ahead_held = list(far), list(outs), list(held)
    plan.ahead_copies = copies
    at = dict(
        zip(
            outs,
            call(
                with_plan(ahead_kernel),
                "ahead",
                list(outs.values()),
                [],
                far=list(far.values()),
                scratch=[VMEM(*kind) for kind in held.values()] + [sems(len(copies))],
                flops=2 * (2 * edges + nodes) * width * width,
                mib=12,
            ),
        )
    )

    (wide,) = call(with_plan(join_kernel), "join", [((kept, width), BF16)], [border, *lat_rows])
    even_rows, odd_rows = [lax.ppermute(wide, axes, pairs) for pairs in plan.lon_pairs]

    near = {
        "count": edge_count,
        "wide": wide,
        "even_rows": even_rows,
        "odd_rows": odd_rows,
        "coarse_rows": coarse_rows,
        **{
            name: at[name]
            for name in (
                "w_edge_mid",
                "edge_part",
                "node_part",
                "sent",
                "received",
                *passed_on,
            )
        },
    }
    far = {
        "edge": edge_feat,
        "w_node_in": w_node_in,
        "w_node_out": w_node_out,
        "cot_node": cot_node,
        "cot_edge": cot_edge,
    }
    copies = {
        "edge": ("edge", None),
        "w_node_low": ("w_node_in", 1),
        "w_node_out": ("w_node_out", None),
        "cot_node": ("cot_node", None),
        "cot_edge": ("cot_edge", None),
        "w_node_top": ("w_node_in", 0),
    }
    plan.main_names, plan.main_copies, plan.main_held = [*near, *far], copies, list(copies)
    outs = [
        ((3 * halo, width), BF16),
        ((2 * nodes, width), BF16),
        ((edges, width), BF16),
        ((nodes, width), F32),
        *[((3 * halo, width), BF16)] * len(plan.lat_pairs),
        (node_feat.shape, BF16),
        (coarse_shape, BF16),
    ]
    kept_grad, agg_grad, edge_dpre, local, *lat_grads, new_nodes, coarse_send = call(
        with_plan(main_kernel),
        "main",
        outs,
        list(near.values()),
        far=list(far.values()),
        scratch=[VMEM((plan.table, width), BF16), VMEM(node_feat.shape, BF16)]
        + [VMEM(coarse_shape, F32), VMEM(coarse_shape, BF16)]
        + [
            VMEM(*(square if part is not None else (far[source].shape, far[source].dtype)))
            for source, part in copies.values()
        ]
        + [sems(len(copies) + 2)],
        flops=2 * 5 * edges * width * width,
        mib=20,
        results=2,
    )

    lat_back = [
        lax.ppermute(grad, axes, pairs) for grad, pairs in zip(lat_grads, plan.lat_pairs)
    ]
    coarse_back = lax.all_to_all(coarse_send, axes, 0, 0, tiled=True)
    mine, even_grad, odd_grad = call(
        with_plan(middle_kernel),
        "middle",
        [((halo, width), F32), ((halo, width), BF16), ((halo, width), BF16)],
        [kept_grad, *lat_back],
    )
    lon_back = [
        lax.ppermute(grad, axes, pairs)
        for grad, pairs in zip((even_grad, odd_grad), plan.lon_pairs)
    ]
    grad_local, grad_edges = call(
        with_plan(behind_kernel),
        "behind",
        [((nodes, width), F32), (edge_feat.shape, BF16)],
        [at["received"], edge_dpre, agg_grad, local, mine],
        far=[w_edge_in, cot_edge],
        scratch=[VMEM(*square), VMEM(*square), *like([cot_edge, edge_feat]), sems(4)],
        flops=2 * (edges + nodes) * width * width,
        mib=8,
        results=1,
    )
    (grad_nodes,) = call(
        with_plan(last_kernel),
        "last",
        [(node_feat.shape, BF16)],
        [grad_local, mine, at["place"], at["at_coarse"], coarse_back, *lon_back],
        results=1,
    )
    return new_nodes, grad_nodes, grad_edges


def solution(mesh):
    lon, lat = mesh.shape["lon"], mesh.shape["lat"]
    cells = lambda rank: P("lon", "lat", *([None] * (rank - 2)))

    def sharded(*args):
        node_feat, edge_feat, halo_list, coarse_list = args[0], args[1], args[5], args[6]
        plan = Plan(
            lon,
            lat,
            node_feat.shape[2],
            edge_feat.shape[2],
            halo_list.shape[2],
            coarse_list.shape[2],
            node_feat.shape[3],
        )
        return body(plan, *args)

    ranks = (4, 4, 3, 3, 2, 3, 3)
    return jax.shard_map(
        sharded,
        mesh=mesh,
        in_specs=tuple(cells(r) for r in ranks) + (P(),) * 10 + (cells(4), cells(4)),
        out_specs=(cells(4), cells(4), cells(4)),
        check_vma=False,
    )
```

```python
import functools

import jax
import jax.numpy as jnp
from jax import lax
from jax.experimental import pallas as pl
from jax.experimental.pallas import tpu as pltpu
from jax.sharding import PartitionSpec as P

F32 = jnp.float32
BF16 = jnp.bfloat16
VMEM = pltpu.VMEM
SENT_ROWS = 128


def dot_nn(a, b):
    return jnp.dot(a, b, preferred_element_type=F32)


def dot_tn(a, b):
    return lax.dot_general(a, b, (((0,), (0,)), ((), ())), preferred_element_type=F32)


def dot_nt(a, b):
    return lax.dot_general(a, b, (((1,), (1,)), ((), ())), preferred_element_type=F32)


def as_one_hot(mask):
    return jnp.where(mask, 1.0, 0.0).astype(BF16)


def one_hot_rows(index_row, rows):
    return lax.broadcasted_iota(jnp.int32, (rows, index_row.shape[1]), 0) == index_row


def live_one_hot(index_row, rows, count):
    lanes = lax.broadcasted_iota(jnp.int32, (rows, index_row.shape[1]), 1)
    return as_one_hot(one_hot_rows(index_row, rows) & (lanes < count))


def in_two(values):
    head = values.astype(BF16)
    tail = (values - head.astype(F32)).astype(BF16)
    return jnp.concatenate([head, tail], axis=0)


def normed_rows(out_rows):
    centre = out_rows - jnp.mean(out_rows, axis=1, keepdims=True)
    inv_std = lax.rsqrt(jnp.mean(centre * centre, axis=1, keepdims=True) + 1e-05)
    return centre * inv_std, inv_std


def norm_backward(grad_norm, normed, inv_std):
    return inv_std * (
        grad_norm
        - jnp.mean(grad_norm, axis=1, keepdims=True)
        - normed * jnp.mean(grad_norm * normed, axis=1, keepdims=True)
    )


def silu_slope(pre, sig):
    return sig * (1.0 + pre * (1.0 - sig))


class Moves:
    def __init__(self, sems):
        self.sems, self.used = sems, 0

    def start(self, source, target):
        copy = pltpu.make_async_copy(source, target, self.sems.at[self.used])
        self.used += 1
        copy.start()
        return copy


class Plan:
    def __init__(self, lon, lat, nodes, edges, halo, owned, width):
        self.lon, self.lat = lon, lat
        self.nodes, self.edges, self.halo, self.owned, self.width = nodes, edges, halo, owned, width
        self.devices = lon * lat
        self.coarse = self.devices * owned
        flat = lambda i, j: (i % lon) * lat + j
        swap = lambda pairs: [p for a, b in pairs for p in ((a, b), (b, a))]
        lat_sets = [
            [(k, k + 1) for k in range(0, lat - 1, 2)],
            [(k, k + 1) for k in range(1, lat - 1, 2)],
        ]
        self.lat_pairs = [
            swap([(flat(i, a), flat(i, b)) for i in range(lon) for a, b in pairs])
            for pairs in lat_sets
            if pairs
        ]
        self.lon_pairs = [
            swap([(flat(i, j), flat(i + 1, j)) for i in range(first, lon, 2) for j in range(lat)])
            for first in (0, 1)
        ]
        self.per_lon = 1 + len(self.lat_pairs)
        self.blocks = 3 * self.per_lon
        self.table = nodes + self.blocks * halo + self.coarse

    def positions(self, sender):
        nodes, halo = self.nodes, self.halo
        lon_odd = lax.rem(lax.axis_index("lon"), 2)
        lat_odd = lax.rem(lax.axis_index("lat"), 2)
        lon_step = [1, 2 - 2 * lon_odd, 2 * lon_odd]
        lat_step = [1, 2 - 2 * lat_odd, 2 * lat_odd][: self.per_lon]
        past = sender - (nodes + 9 * halo)
        if self.owned > 1:
            past = jnp.where(
                past >= 0, lax.rem(past, self.owned) * self.devices + past // self.owned, past
            )
        found = jnp.where(past >= 0, past + (nodes + self.blocks * halo), sender)
        place = 0
        for a in lon_step:
            for b in lat_step:
                row = sender - (nodes + (3 * a + b) * halo)
                inside = (row >= 0) & (row < halo) & (sender >= nodes)
                found = jnp.where(inside, row + (nodes + place * halo), found)
                place += 1
        return found


def pack_kernel(plan, node, halo_list, coarse_list, border, coarse, node_s, halo_s, list_s, sems):
    moves = Moves(sems)
    pairs = ((coarse_list, list_s), (halo_list, halo_s), (node, node_s))
    for copy in [moves.start(*pair) for pair in pairs]:
        copy.wait()
    rows = node_s[0, 0]
    pick = as_one_hot(one_hot_rows(halo_s[0], plan.nodes))
    border[: plan.halo] = dot_tn(pick, rows).astype(BF16)
    own = dot_tn(as_one_hot(one_hot_rows(list_s[0], plan.nodes)), rows)
    parts = plan.width // 128
    pieces = [
        own[k : k + 1, q * 128 : (q + 1) * 128] for k in range(plan.owned) for q in range(parts)
    ]
    coarse[...] = jnp.broadcast_to(jnp.concatenate(pieces, axis=0)[None], coarse.shape)


def block_of(ref, part, width):
    return ref if part is None else ref.at[pl.ds(part * width, width)]


def ahead_kernel(plan, *refs):
    operands = dict(zip(plan.ahead_in, refs))
    refs = refs[len(plan.ahead_in) :]
    held = dict(zip(plan.ahead_out, refs))
    sems = refs[-1]
    held.update(zip(plan.ahead_held, refs[len(plan.ahead_out) : -1]))
    moves = Moves(sems)
    width, nodes = plan.width, plan.nodes
    copies = {
        name: moves.start(block_of(operands[source], part, width), held[name])
        for name, (source, part) in plan.ahead_copies.items()
    }

    def got(name):
        if name in copies:
            copies.pop(name).wait()
        return held[name]

    count = got("count")[...]
    received = live_one_hot(got("receivers")[0], nodes, count)
    held["received"][...] = received
    held["sent"][...] = as_one_hot(
        one_hot_rows(plan.positions(got("senders")[0]), plan.table)
    )
    place = as_one_hot(one_hot_rows(got("halo_list")[0], nodes))
    held["place"][...] = jnp.concatenate([place, place], axis=1)
    at_coarse = one_hot_rows(got("coarse_list")[0], nodes)
    held["at_coarse"][...] = jnp.where(at_coarse, 1.0, 0.0).astype(F32)
    rows = got("node")[0, 0]
    at_receiver = dot_tn(received, rows).astype(BF16)
    held["edge_part"][...] = (
        dot_nn(got("edge")[0, 0], got("w_edge_top")[...])
        + dot_nn(at_receiver, got("w_edge_low")[...])
        + got("b_edge_in")[...]
    )
    held["node_part"][...] = dot_nn(rows, got("w_node_top")[...]) + got("b_node_in")[...]
    for copy in copies.values():
        copy.wait()


def join_kernel(plan, *refs):
    for k, part in enumerate(refs[:-1]):
        refs[-1][k * plan.halo : (k + 1) * plan.halo] = part[: plan.halo]


def edge_cotangent(cot_edge, received, agg_grad):
    twice = jnp.concatenate([received, received], axis=0)
    return cot_edge[0, 0].astype(F32) + dot_tn(twice, agg_grad)


def main_kernel(plan, *refs):
    here = dict(zip(plan.main_names, refs))
    refs = refs[len(plan.main_names) :]
    kept_grad, agg_out, edge_dpre_out, local = refs[:4]
    lat_grads, refs = refs[4 : 3 + plan.per_lon], refs[3 + plan.per_lon :]
    new_nodes, coarse_grad, table, new_s, tiles, coarse_s = refs[:6]
    sems, held = refs[-1], dict(zip(plan.main_held, refs[6:-1]))
    nodes, halo, width = plan.nodes, plan.halo, plan.width
    sent, received = here["sent"], here["received"][...]
    live = jnp.where(
        lax.broadcasted_iota(jnp.int32, (plan.edges, 1), 0) < here["count"][0, 0], 1.0, 0.0
    ).astype(F32)
    moves = Moves(sems)
    copies = {
        name: moves.start(block_of(here[source], part, width), held[name])
        for name, (source, part) in plan.main_copies.items()
    }

    def got(name):
        if name in copies:
            copies.pop(name).wait()
        return held[name] if name in held else here[name]

    start = nodes
    table[:nodes] = got("node")[0, 0]
    for name in ("wide", "even_rows", "odd_rows"):
        rim = plan.per_lon * halo
        table[start : start + rim] = got(name)[:rim]
        start += rim
    parts = width // 128
    for k in range(plan.owned):
        for q in range(parts):
            table[start : start + plan.devices, q * 128 : (q + 1) * 128] = got("coarse_rows")[
                :, k * parts + q, :
            ].astype(BF16)
        start += plan.devices

    w_edge_mid = got("w_edge_mid")[...]
    at_sender = dot_tn(sent[...], table[...]).astype(BF16)
    edge_pre = got("edge_part")[...] + dot_nn(at_sender, w_edge_mid)
    edge_sig = jax.nn.sigmoid(edge_pre)
    edge_out = dot_nn((edge_pre * edge_sig).astype(BF16), got("w_edge_out")[...])
    edge_normed, edge_rstd = normed_rows(edge_out)
    edge_upd = edge_normed * got("gain_edge")[...] + got("shift_edge")[...]
    new_edge = (got("edge")[0, 0].astype(F32) + live * edge_upd).astype(BF16)
    aggregated = dot_nn(received, new_edge).astype(BF16)

    node_pre = got("node_part")[...] + dot_nn(aggregated, got("w_node_low")[...])
    node_sig = jax.nn.sigmoid(node_pre)
    node_out = dot_nn((node_pre * node_sig).astype(BF16), got("w_node_out")[...])
    node_normed, node_rstd = normed_rows(node_out)
    node_upd = node_normed * got("gain_node")[...] + got("shift_node")[...]
    new_s[0, 0] = (got("node")[0, 0].astype(F32) + node_upd).astype(BF16)
    leaving = moves.start(new_s, new_nodes)

    node_dout = norm_backward(
        got("cot_node")[0, 0].astype(F32) * got("gain_node")[...], node_normed, node_rstd
    ).astype(BF16)
    node_dpre = (
        dot_nt(node_dout, got("w_node_out")[...]) * silu_slope(node_pre, node_sig)
    ).astype(BF16)
    agg_grad = in_two(dot_nt(node_dpre, got("w_node_low")[...]))
    agg_out[...] = agg_grad
    edge_cot = edge_cotangent(got("cot_edge"), received, agg_grad)

    edge_dout = norm_backward(
        live * edge_cot * got("gain_edge")[...], edge_normed, edge_rstd
    ).astype(BF16)
    edge_dpre = (
        dot_nt(edge_dout, got("w_edge_out")[...]) * silu_slope(edge_pre, edge_sig)
    ).astype(BF16)
    edge_dpre_out[...] = edge_dpre
    away = dot_nn(sent[...], edge_dpre).astype(BF16)
    kept = plan.per_lon * halo
    rim_end = nodes + 3 * kept
    coarse_sum = dot_nt(away[rim_end:], w_edge_mid)
    for k in range(plan.owned):
        for q in range(parts):
            tiles[:, k * parts + q, :] = coarse_sum[
                k * plan.devices : (k + 1) * plan.devices, q * 128 : (q + 1) * 128
            ]
    coarse_s[...] = tiles[...].astype(BF16)
    coarse_leaving = moves.start(coarse_s, coarse_grad)
    away_grad = dot_nt(away[:rim_end], w_edge_mid)
    own_grad, away_grad = away_grad[:nodes], away_grad[nodes:]
    for a in range(3):
        rows = slice(a * halo, (a + 1) * halo)
        kept_grad[rows] = away_grad[a * kept : a * kept + halo].astype(BF16)
        for k, lat_grad in enumerate(lat_grads):
            first = a * kept + (k + 1) * halo
            lat_grad[rows] = away_grad[first : first + halo].astype(BF16)
    local[...] = (
        got("cot_node")[0, 0].astype(F32) + dot_nt(node_dpre, got("w_node_top")[...]) + own_grad
    )
    leaving.wait()
    coarse_leaving.wait()


def behind_kernel(plan, *refs):
    received, edge_dpre, agg_grad, local, _, w_edge_in, cot_edge, grad_local, grad_edges = refs[:9]
    w_top_s, w_low_s, cot_s, grad_s, sems = refs[9:]
    moves, width = Moves(sems), plan.width
    top = moves.start(block_of(w_edge_in, 0, width), w_top_s)
    cot = moves.start(cot_edge, cot_s)
    low = moves.start(block_of(w_edge_in, 2, width), w_low_s)
    dpre = edge_dpre[...]
    at_receiver = dot_nn(received[...], dpre).astype(BF16)
    cot.wait()
    edge_cot = edge_cotangent(cot_s, received[...], agg_grad[...])
    top.wait()
    grad_s[0, 0] = (edge_cot + dot_nt(dpre, w_top_s[...])).astype(BF16)
    leaving = moves.start(grad_s, grad_edges)
    low.wait()
    grad_local[...] = local[...] + dot_nt(at_receiver, w_low_s[...])
    leaving.wait()


def middle_kernel(plan, kept, *refs):
    total = kept[...].astype(F32)
    for part in refs[:-3]:
        total = total + part[...].astype(F32)
    mine, even, odd = refs[-3:]
    halo = plan.halo
    mine[...] = total[:halo]
    even[...] = total[halo : 2 * halo].astype(BF16)
    odd[...] = total[2 * halo :].astype(BF16)


def last_kernel(plan, *refs):
    grad_local, mine, place, at_coarse, coarse = refs[:5]
    out = refs[-1]
    total = mine[...]
    for part in refs[5:-1]:
        total = total + part[...].astype(F32)
    result = grad_local[...] + dot_nn(place[...], in_two(total))
    share = jnp.sum(coarse[...].astype(F32), axis=0)
    parts = plan.width // 128
    for k in range(plan.owned):
        row = jnp.concatenate([share[k * parts + q : k * parts + q + 1] for q in range(parts)], axis=1)
        result = result + at_coarse[:, k : k + 1] * row
    out[0, 0] = result.astype(BF16)


def call(body, name, outs, operands, far=(), scratch=(), flops=0, mib=4, results=0):
    whole = pl.BlockSpec(memory_space=VMEM)
    scalars = pl.BlockSpec(memory_space=pltpu.SMEM)
    anywhere = pl.BlockSpec(memory_space=pl.ANY)
    far = [pltpu.with_memory_space_constraint(a, pltpu.HBM) if a.size > 1 else a for a in far]
    moved = sum(a.size * a.dtype.itemsize for a in (*operands, *far))
    near = len(outs) - results
    return pl.pallas_call(
        body,
        name=name,
        out_shape=[VMEM(shape, dtype) for shape, dtype in outs[:near]]
        + [jax.ShapeDtypeStruct(shape, dtype) for shape, dtype in outs[near:]],
        in_specs=[scalars if a.size == 1 else whole for a in operands] + [anywhere] * len(far),
        out_specs=[whole] * near + [anywhere if scratch else whole] * results,
        scratch_shapes=list(scratch),
        compiler_params=pltpu.CompilerParams(vmem_limit_bytes=mib * 1024 * 1024),
        cost_estimate=pl.CostEstimate(flops=flops, bytes_accessed=moved, transcendentals=0),
    )(*operands, *far)


def like(arrays):
    return [VMEM(a.shape, a.dtype) for a in arrays]


def sems(count):
    return pltpu.SemaphoreType.DMA((count,))


def body(
    plan,
    node_feat,
    edge_feat,
    senders,
    receivers,
    edge_count,
    halo_list,
    coarse_list,
    w_edge_in,
    b_edge_in,
    w_edge_out,
    gain_edge,
    shift_edge,
    w_node_in,
    b_node_in,
    w_node_out,
    gain_node,
    shift_node,
    cot_node,
    cot_edge,
):
    axes = ("lon", "lat")
    halo, width, nodes, edges = plan.halo, plan.width, plan.nodes, plan.edges
    row = lambda vec: vec.reshape(1, width)
    with_plan = lambda kernel: functools.partial(kernel, plan)
    coarse_shape = (plan.devices, plan.owned * width // 128, 128)
    kept = plan.per_lon * halo

    operands = [node_feat, halo_list, coarse_list]
    border, coarse_out = call(
        with_plan(pack_kernel),
        "pack",
        [((max(halo, SENT_ROWS), width), BF16), (coarse_shape, F32)],
        [],
        far=operands,
        scratch=like(operands) + [sems(3)],
    )
    coarse_rows = lax.all_to_all(coarse_out, axes, 0, 0, tiled=True)
    lat_rows = [lax.ppermute(border, axes, pairs) for pairs in plan.lat_pairs]

    far = {
        "edge": edge_feat,
        "w_edge_in": w_edge_in,
        "count": edge_count,
        "receivers": receivers,
        "node": node_feat,
        "b_edge_in": row(b_edge_in),
        "senders": senders,
        "halo_list": halo_list,
        "coarse_list": coarse_list,
        "w_node_in": w_node_in,
        "b_node_in": row(b_node_in),
        "w_edge_out": w_edge_out,
        "gain_edge": row(gain_edge),
        "shift_edge": row(shift_edge),
        "gain_node": row(gain_node),
        "shift_node": row(shift_node),
    }
    square = ((width, width), BF16)
    copies = {name: (name, None) for name in far if name not in ("w_edge_in", "w_node_in")}
    copies["w_edge_top"] = ("w_edge_in", 0)
    copies["w_edge_low"] = ("w_edge_in", 2)
    copies["w_node_top"] = ("w_node_in", 0)
    copies["w_edge_mid"] = ("w_edge_in", 1)
    passed_on = ("node", "w_edge_out", "gain_edge", "shift_edge", "gain_node", "shift_node")
    outs = {
        **{name: (far[name].shape, far[name].dtype) for name in passed_on},
        "w_edge_mid": square,
        "edge_part": ((edges, width), F32),
        "node_part": ((nodes, width), F32),
        "sent": ((plan.table, edges), BF16),
        "received": ((nodes, edges), BF16),
        "place": ((nodes, 2 * halo), BF16),
        "at_coarse": ((nodes, plan.owned), F32),
    }
    held = {
        name: square if part is not None else (far[source].shape, far[source].dtype)
        for name, (source, part) in copies.items()
        if name not in outs
    }
    plan.ahead_in, plan.ahead_out, plan.ahead_held = list(far), list(outs), list(held)
    plan.ahead_copies = copies
    at = dict(
        zip(
            outs,
            call(
                with_plan(ahead_kernel),
                "ahead",
                list(outs.values()),
                [],
                far=list(far.values()),
                scratch=[VMEM(*kind) for kind in held.values()] + [sems(len(copies))],
                flops=2 * (2 * edges + nodes) * width * width,
                mib=12,
            ),
        )
    )

    (wide,) = call(with_plan(join_kernel), "join", [((kept, width), BF16)], [border, *lat_rows])
    even_rows, odd_rows = [lax.ppermute(wide, axes, pairs) for pairs in plan.lon_pairs]

    near = {
        "count": edge_count,
        "wide": wide,
        "even_rows": even_rows,
        "odd_rows": odd_rows,
        "coarse_rows": coarse_rows,
        **{
            name: at[name]
            for name in (
                "w_edge_mid",
                "edge_part",
                "node_part",
                "sent",
                "received",
                *passed_on,
            )
        },
    }
    far = {
        "edge": edge_feat,
        "w_node_in": w_node_in,
        "w_node_out": w_node_out,
        "cot_node": cot_node,
        "cot_edge": cot_edge,
    }
    copies = {
        "edge": ("edge", None),
        "w_node_low": ("w_node_in", 1),
        "w_node_out": ("w_node_out", None),
        "cot_node": ("cot_node", None),
        "cot_edge": ("cot_edge", None),
        "w_node_top": ("w_node_in", 0),
    }
    plan.main_names, plan.main_copies, plan.main_held = [*near, *far], copies, list(copies)
    outs = [
        ((3 * halo, width), BF16),
        ((2 * nodes, width), BF16),
        ((edges, width), BF16),
        ((nodes, width), F32),
        *[((3 * halo, width), BF16)] * len(plan.lat_pairs),
        (node_feat.shape, BF16),
        (coarse_shape, BF16),
    ]
    kept_grad, agg_grad, edge_dpre, local, *lat_grads, new_nodes, coarse_send = call(
        with_plan(main_kernel),
        "main",
        outs,
        list(near.values()),
        far=list(far.values()),
        scratch=[VMEM((plan.table, width), BF16), VMEM(node_feat.shape, BF16)]
        + [VMEM(coarse_shape, F32), VMEM(coarse_shape, BF16)]
        + [
            VMEM(*(square if part is not None else (far[source].shape, far[source].dtype)))
            for source, part in copies.values()
        ]
        + [sems(len(copies) + 2)],
        flops=2 * 5 * edges * width * width,
        mib=20,
        results=2,
    )

    lat_back = [
        lax.ppermute(grad, axes, pairs) for grad, pairs in zip(lat_grads, plan.lat_pairs)
    ]
    coarse_back = lax.all_to_all(coarse_send, axes, 0, 0, tiled=True)
    mine, even_grad, odd_grad = call(
        with_plan(middle_kernel),
        "middle",
        [((halo, width), F32), ((halo, width), BF16), ((halo, width), BF16)],
        [kept_grad, *lat_back],
    )
    lon_back = [
        lax.ppermute(grad, axes, pairs)
        for grad, pairs in zip((even_grad, odd_grad), plan.lon_pairs)
    ]
    grad_local, grad_edges = call(
        with_plan(behind_kernel),
        "behind",
        [((nodes, width), F32), (edge_feat.shape, BF16)],
        [at["received"], edge_dpre, agg_grad, local, mine],
        far=[w_edge_in, cot_edge],
        scratch=[VMEM(*square), VMEM(*square), *like([cot_edge, edge_feat]), sems(4)],
        flops=2 * (edges + nodes) * width * width,
        mib=8,
        results=1,
    )
    (grad_nodes,) = call(
        with_plan(last_kernel),
        "last",
        [(node_feat.shape, BF16)],
        [grad_local, mine, at["place"], at["at_coarse"], coarse_back, *lon_back[::-1]],
        results=1,
    )
    return new_nodes, grad_nodes, grad_edges


def solution(mesh):
    lon, lat = mesh.shape["lon"], mesh.shape["lat"]
    cells = lambda rank: P("lon", "lat", *([None] * (rank - 2)))

    def sharded(*args):
        node_feat, edge_feat, halo_list, coarse_list = args[0], args[1], args[5], args[6]
        plan = Plan(
            lon,
            lat,
            node_feat.shape[2],
            edge_feat.shape[2],
            halo_list.shape[2],
            coarse_list.shape[2],
            node_feat.shape[3],
        )
        return body(plan, *args)

    ranks = (4, 4, 3, 3, 2, 3, 3)
    return jax.shard_map(
        sharded,
        mesh=mesh,
        in_specs=tuple(cells(r) for r in ranks) + (P(),) * 10 + (cells(4), cells(4)),
        out_specs=(cells(4), cells(4), cells(4)),
        check_vma=False,
    )
```
